32 devices in a mesh: seq: 8 (over z, y), head: 4 (over x, core).
Axes of the slice: x: 2, y: 2, z: 4, core: 2. Of those that a mesh axis runs over, the one named last changes fastest.
Arguments:
- query_in: bfloat16 [2048, 4096], P('seq', 'head'), may hold values from -6 to 6
- key_in: bfloat16 [2048, 4096], P('seq', 'head'), may hold values from -6 to 6
- value_in: bfloat16 [2048, 4096], P('seq', 'head')
- out_grad: bfloat16 [2048, 4096], P('seq', 'head'), may hold values from -6 to 6
- norm_gain: float32 [4096], P('head'), may hold values from 0.5 to 1.5
- doc_ids: int32 [2048], P('seq'), may hold values from 0 to 7, as said below
- start_group: int32 [8], replicated, may hold values from 0 to 6, as said below
Outputs:
- normed: bfloat16 [2048, 4096], P('seq', 'head')
- grad_query: bfloat16 [2048, 4096], P('seq', 'head')
- grad_key: bfloat16 [2048, 4096], P('seq', 'head')
- grad_value: bfloat16 [2048, 4096], P('seq', 'head')
The draws below stay inside these ranges and needn't reach their ends.
Inputs may be any that keep to these rules, and one draw needn't show every extreme that they name: `doc_ids`: 0 at the first token, never falling, one more at each document start. `start_group`: entry c is the block in which the document holding block c's first token begins; it agrees with doc_ids.
All inputs are finite; a program needn't handle non-finite values.
Results may differ from the reference program's by a relative error of at most 0.0058.
Values may be sent and summed in bfloat16 or wider, within the bound.
No kernel may reach another device: no remote copies, remote signals or barrier semaphores. Data moves between devices by JAX's collectives and lax.ppermute only.
A program may use at most 128 MiB of HBM per device.

```python
import math
from functools import partial
import jax
import jax.numpy as jnp
from jax import lax

H = 32
HD = 128
TOK_DEV = 256
GROUPS = 8
TOKENS = 2048


def doc_layout(key):
    base = jax.random.fold_in(key, 7)
    places_all = jnp.arange(TOKENS, dtype=jnp.int32)
    priority = jax.random.permutation(jax.random.fold_in(base, 1), TOKENS).astype(jnp.int32)
    other_block = jax.random.randint(jax.random.fold_in(base, 2), (1,), 2, max(GROUPS - 2, 3))
    aligned = jnp.concatenate([jnp.full((1,), GROUPS - 2, jnp.int32), other_block.astype(jnp.int32)]) * TOK_DEV
    boost = jnp.zeros((TOKENS,), jnp.int32).at[aligned].set(TOKENS)
    forbidden = (places_all == 0) | (places_all == TOK_DEV) | (places_all >= (GROUPS - 1) * TOK_DEV)
    priority = jnp.where(forbidden, -1, priority + boost)
    chosen = lax.top_k(priority, GROUPS // 2 + 3)[1]
    marks = jnp.zeros((TOKENS,), jnp.int32).at[chosen].set(1)
    doc_ids = jnp.cumsum(marks).astype(jnp.int32)
    places = jnp.where(marks > 0, places_all, 0)
    begins = lax.cummax(places, axis=0)
    start_group = (begins[::TOK_DEV] // TOK_DEV).astype(jnp.int32)
    return (doc_ids, start_group)


def draw_doc_ids(key, part):
    return doc_layout(key)[0]


def draw_start_group(key, part):
    return doc_layout(key)[1]


def draw_value_in(key, part):
    width = H * HD
    columns = jnp.arange(width, dtype=jnp.float32) / (width - 1)
    noise = jax.random.normal(jax.random.fold_in(key, 1), (TOKENS, width), jnp.float32)
    ramp = 3.0 ** (0.5 * columns)
    col_scale = jnp.exp(jax.random.uniform(jax.random.fold_in(key, 2), (width,), jnp.float32, 0.0, math.log(10.0)))
    row_scale = jnp.exp(jax.random.uniform(jax.random.fold_in(key, 3), (TOKENS, 1), jnp.float32, 0.0, math.log(10.0)))
    return (noise * col_scale * row_scale * ramp * 0.25).astype(jnp.bfloat16)


def steps_of(own_key, shape, cuts, low, top_value):
    def one(position, shards_of):
        draws = jax.random.uniform(jax.random.fold_in(jax.random.fold_in(own_key, 6), position), (shards_of,), jnp.float32, low / len(cuts), top_value / len(cuts))
        return jnp.repeat(jnp.exp(draws), shape[position] // shards_of).reshape((-1,) + (1,) * (len(shape) - position - 1))

    gain = one(*cuts[0])
    for cut in cuts[1:]:
        gain = gain * one(*cut)
    return gain


def bell_draw(rng, shape, deviation, limit, cuts=(), held_as=jnp.bfloat16):
    values = deviation * jax.random.normal(rng, shape, jnp.float32)
    if cuts:
        values = values * steps_of(rng, shape, cuts, -0.22, 0.18)
    return jnp.clip(values, -limit, limit).astype(held_as)


def setup_inputs(seed: int = 0) -> dict:
    streams_of = jax.random.split(jax.random.key(seed), 8)
    return {
        "query_in": bell_draw(streams_of[0], (TOKENS, H * HD), 1.0, 6.0, ((0, 8), (1, 4))),
        "key_in": bell_draw(streams_of[1], (TOKENS, H * HD), 1.0, 6.0, ((0, 8), (1, 4))),
        "value_in": draw_value_in(jax.random.fold_in(streams_of[7], 71), 0),
        "out_grad": bell_draw(streams_of[3], (TOKENS, H * HD), 1.0, 6.0, ((0, 8), (1, 4))),
        "norm_gain": jnp.clip(1.0 + 0.1 * jax.random.normal(streams_of[4], (H * HD,), jnp.float32), 0.5, 1.5),
        "doc_ids": draw_doc_ids(jax.random.fold_in(streams_of[7], 71), 0),
        "start_group": draw_start_group(jax.random.fold_in(streams_of[7], 71), 0),
    }


epsilon = 1e-06
contract = partial(jnp.einsum, precision=lax.Precision.HIGHEST)

def reference(query_in, key_in, value_in, out_grad, norm_gain, doc_ids, start_group):
    width = H * HD

    def blocked(array):
        return array.reshape(GROUPS, TOK_DEV, H, HD)
    query_b = blocked(query_in)
    key_b = blocked(key_in)
    value_b = blocked(value_in)
    grad_b = blocked(out_grad)
    ids_b = doc_ids.reshape(GROUPS, TOK_DEV)
    first_doc = (ids_b == ids_b[:, :1]).astype(jnp.float32)
    last_doc = (ids_b == ids_b[:, -1:]).astype(jnp.float32)
    group_ids = jnp.arange(GROUPS, dtype=jnp.int32)
    causal = jnp.arange(TOK_DEV)[:, None] >= jnp.arange(TOK_DEV)[None, :]
    gain_heads = norm_gain.reshape(H, HD).astype(jnp.float32)

    def tail_of(pieces):
        key_c, value_c, last_c = pieces
        return contract('tha,thb->hab', key_c.astype(jnp.float32) * last_c[:, None, None], value_c.astype(jnp.float32))
    tails = lax.map(tail_of, (key_b, value_b, last_doc))
    forward_mask = ((start_group[:, None] <= group_ids[None, :]) & (group_ids[None, :] < group_ids[:, None])).astype(jnp.float32)
    carries = contract('cj,jhab->chab', forward_mask, tails).astype(jnp.bfloat16)

    def attention_weights(query_f, key_f, ids_c):
        same_doc = causal & (ids_c[:, None] == ids_c[None, :])
        scores = contract('tha,uha->htu', query_f, key_f)
        return (jnp.where(same_doc[None], scores, 0.0).astype(jnp.bfloat16), same_doc)

    def forward_block(pieces):
        query_c, key_c, value_c, grad_c, ids_c, first_c, carry_c = pieces
        query_f = query_c.astype(jnp.float32)
        key_f = key_c.astype(jnp.float32)
        value_f = value_c.astype(jnp.float32)
        grad_f = grad_c.astype(jnp.float32)
        weights, same_doc = attention_weights(query_f, key_f, ids_c)
        attended = contract('htu,uhb->thb', weights.astype(jnp.float32), value_f)
        attended = attended + first_c[:, None, None] * contract('tha,hab->thb', query_f, carry_c.astype(jnp.float32))
        square_total = lax.optimization_barrier(jnp.sum(attended * attended, axis=(1, 2)))
        inverse_rms = lax.rsqrt(square_total / width + epsilon)
        normed = (attended * inverse_rms[:, None, None] * gain_heads).astype(jnp.bfloat16)
        cross_total = lax.optimization_barrier(jnp.sum(gain_heads * grad_f * attended, axis=(1, 2)))
        grad_attended = (inverse_rms[:, None, None] * gain_heads * grad_f - (inverse_rms ** 3 * cross_total / width)[:, None, None] * attended).astype(jnp.bfloat16)
        head_state = contract('tha,thb->hab', query_f * first_c[:, None, None], grad_attended.astype(jnp.float32))
        return (normed, grad_attended, head_state)
    normed, grad_att, heads = lax.map(forward_block, (query_b, key_b, value_b, grad_b, ids_b, first_doc, carries))
    backward_mask = ((start_group[None, :] <= group_ids[:, None]) & (group_ids[:, None] < group_ids[None, :])).astype(jnp.float32)
    dstates = contract('cj,jhab->chab', backward_mask, heads).astype(jnp.bfloat16)

    def backward_block(pieces):
        query_c, key_c, value_c, grad_c, ids_c, first_c, last_c, carry_c, dstate_c = pieces
        query_f = query_c.astype(jnp.float32)
        key_f = key_c.astype(jnp.float32)
        value_f = value_c.astype(jnp.float32)
        grad_f = grad_c.astype(jnp.float32)
        carry_f = carry_c.astype(jnp.float32)
        dstate_f = dstate_c.astype(jnp.float32)
        weights, same_doc = attention_weights(query_f, key_f, ids_c)
        grad_scores = jnp.where(same_doc[None], contract('tha,uha->htu', grad_f, value_f), 0.0).astype(jnp.bfloat16).astype(jnp.float32)
        grad_q = contract('htu,uha->tha', grad_scores, key_f) + first_c[:, None, None] * contract('thb,hab->tha', grad_f, carry_f)
        grad_k = contract('htu,tha->uha', grad_scores, query_f) + last_c[:, None, None] * contract('uhb,hab->uha', value_f, dstate_f)
        grad_v = contract('htu,thb->uhb', weights.astype(jnp.float32), grad_f) + last_c[:, None, None] * contract('uha,hab->uhb', key_f, dstate_f)
        return (grad_q.astype(jnp.bfloat16), grad_k.astype(jnp.bfloat16), grad_v.astype(jnp.bfloat16))
    grad_q, grad_k, grad_v = lax.map(backward_block, (query_b, key_b, value_b, grad_att, ids_b, first_doc, last_doc, carries, dstates))
    shape = (TOKENS, width)
    return (normed.reshape(shape), grad_q.reshape(shape), grad_k.reshape(shape), grad_v.reshape(shape))
```

```python
import functools

import jax
import jax.numpy as jnp
from jax import lax
from jax.experimental import pallas as pl
from jax.experimental.pallas import tpu as pltpu
from jax.sharding import PartitionSpec as P

H = 32
HD = 128
WIDTH = H * HD

epsilon = 1e-06

f32 = jnp.float32
bf16 = jnp.bfloat16


def dot(a, b, da, db):
    return lax.dot_general(a, b, (((da,), (db,)), ((), ())), preferred_element_type=f32)


def head_cols(h):
    return slice(h * HD, (h + 1) * HD)


def column(row):
    n = row.shape[1]
    at = lax.broadcasted_iota(jnp.int32, (n, n), 0) == lax.broadcasted_iota(jnp.int32, (n, n), 1)
    return jnp.sum(jnp.where(at, row, 0.0), axis=1, keepdims=True)


def as_row(col):
    n = col.shape[0]
    at = lax.broadcasted_iota(jnp.int32, (n, n), 0) == lax.broadcasted_iota(jnp.int32, (n, n), 1)
    return jnp.sum(jnp.where(at, col, 0.0), axis=0, keepdims=True)


def ids_of(ids_ref):
    row = ids_ref[...].astype(f32)
    return row, column(row)


def first_of(row, col):
    return (col == row[:, :1]).astype(f32)


def last_of(row, col):
    return (col == row[:, -1:]).astype(f32)


def wide(col, dtype=bf16):
    return jnp.broadcast_to(col, (col.shape[0], HD)).astype(dtype)


def tail_kernel(ids_ref, k_ref, v_ref, tail_ref):
    row, col = ids_of(ids_ref)
    last = wide(last_of(row, col))
    for h in range(tail_ref.shape[0]):
        tail_ref[h] = dot(k_ref[:, head_cols(h)] * last, v_ref[:, head_cols(h)], 0, 0).astype(bf16)


def local_kernel(ids_ref, q_ref, k_ref, v_ref, att_ref):
    row, col = ids_of(ids_ref)
    n = row.shape[1]
    t = lax.broadcasted_iota(jnp.int32, (n, n), 0)
    u = lax.broadcasted_iota(jnp.int32, (n, n), 1)
    same = (u <= t) & (col == row)
    for h in range(q_ref.shape[1] // HD):
        c = head_cols(h)
        w = jnp.where(same, dot(q_ref[:, c], k_ref[:, c], 1, 1), 0.0).astype(bf16)
        att_ref[:, c] = dot(w, v_ref[:, c], 1, 0)


def attend_kernel(ids_ref, att_ref, q_ref, g_ref, gain_ref, carry_ref, out_ref, sums_ref):
    row, col = ids_of(ids_ref)
    first = wide(first_of(row, col))
    square = jnp.zeros((row.shape[1], HD), f32)
    cross = jnp.zeros((row.shape[1], HD), f32)
    for h in range(q_ref.shape[1] // HD):
        c = head_cols(h)
        att = att_ref[:, c] + dot(q_ref[:, c] * first, carry_ref[h], 1, 0)
        out_ref[:, c] = att
        square = square + att * att
        cross = cross + gain_ref[:, c] * g_ref[:, c].astype(f32) * att
    sums_ref[0:1, :] = as_row(jnp.sum(square, axis=1, keepdims=True))
    sums_ref[1:2, :] = as_row(jnp.sum(cross, axis=1, keepdims=True))


def scales(sum_refs):
    total = sum_refs[0][...]
    for ref in sum_refs[1:]:
        total = total + ref[...]
    inverse = lax.rsqrt(total[0:1] / WIDTH + epsilon)
    pull = inverse * inverse * inverse * total[1:2] / WIDTH
    return inverse, pull


def grad_kernel(n_sums, ids_ref, att_ref, q_ref, g_ref, gain_ref, *refs):
    sum_refs, (grad_ref, head_ref) = refs[:n_sums], refs[n_sums:]
    row, col = ids_of(ids_ref)
    first = wide(first_of(row, col))
    inverse, pull = scales(sum_refs)
    inverse, pull = column(inverse), column(pull)
    for h in range(q_ref.shape[1] // HD):
        c = head_cols(h)
        grad = (inverse * gain_ref[:, c] * g_ref[:, c].astype(f32) - pull * att_ref[:, c]).astype(bf16)
        grad_ref[:, c] = grad
        head_ref[h] = dot(q_ref[:, c] * first, grad, 0, 0).astype(bf16)


def back_kernel(n_sums, ids_ref, att_ref, q_ref, k_ref, v_ref, grad_ref, gain_ref, carry_ref, *refs):
    sum_refs, (normed_ref, gq_ref, gk_ref, gv_ref) = refs[:n_sums], refs[n_sums:]
    row, col = ids_of(ids_ref)
    first = wide(first_of(row, col))
    n = row.shape[1]
    inverse = column(scales(sum_refs)[0])
    t = lax.broadcasted_iota(jnp.int32, (n, n), 0)
    u = lax.broadcasted_iota(jnp.int32, (n, n), 1)
    same = (u <= t) & (col == row)
    same_t = (t <= u) & (col == row)
    for h in range(q_ref.shape[1] // HD):
        c = head_cols(h)
        q, k, v, grad = q_ref[:, c], k_ref[:, c], v_ref[:, c], grad_ref[:, c]
        normed_ref[:, c] = (att_ref[:, c] * inverse * gain_ref[:, c]).astype(bf16)
        gs = jnp.where(same, dot(grad, v, 1, 1), 0.0).astype(bf16)
        gq_ref[:, c] = (dot(gs, k, 1, 0) + dot(grad * first, carry_ref[h], 1, 1)).astype(bf16)
        gs_t = jnp.where(same_t, dot(v, grad, 1, 1), 0.0).astype(bf16)
        gk_ref[:, c] = dot(gs_t, q, 1, 0)
        w_t = jnp.where(same_t, dot(k, q, 1, 1), 0.0).astype(bf16)
        gv_ref[:, c] = dot(w_t, grad, 1, 0)


def last_kernel(ids_ref, k_ref, v_ref, gk_in, gv_in, back_ref, gk_ref, gv_ref):
    row, col = ids_of(ids_ref)
    last = wide(last_of(row, col))
    for h in range(k_ref.shape[1] // HD):
        c = head_cols(h)
        back = back_ref[h]
        gk_ref[:, c] = (gk_in[:, c] + dot(v_ref[:, c] * last, back, 1, 1)).astype(bf16)
        gv_ref[:, c] = (gv_in[:, c] + dot(k_ref[:, c] * last, back, 1, 0)).astype(bf16)


def call(kernel, outs, flops, *args):
    moved = sum(a.size * a.dtype.itemsize for a in (*args, *outs))
    return pl.pallas_call(
        kernel,
        out_shape=outs,
        cost_estimate=pl.CostEstimate(flops=flops, bytes_accessed=moved, transcendentals=0),
        compiler_params=pltpu.CompilerParams(vmem_limit_bytes=32 * 2**20),
    )(*args)


def spread(state, mask, groups):
    shape = state.shape
    pieces = state.reshape(groups, -1, shape[-1])
    here = lax.all_to_all(pieces, "seq", 0, 0)
    sums = jnp.einsum("cj,jmn->cmn", mask.astype(bf16), here, preferred_element_type=f32)
    return lax.all_to_all(sums.astype(bf16), "seq", 0, 0).reshape(shape)


def over_head(sums):
    size = lax.axis_size("head")
    power = size & (size - 1) == 0
    return [sums] + [
        lax.ppermute(sums, "head", [(i, i ^ k if power else (i + k) % size) for i in range(size)])
        for k in range(1, size)
    ]


def local(query_in, key_in, value_in, out_grad, norm_gain, doc_ids, start_group):
    n, cols = query_in.shape
    heads = cols // HD
    groups = lax.axis_size("seq")
    ids = doc_ids.reshape(1, n)
    gain = norm_gain.reshape(1, cols)
    group_ids = jnp.arange(groups, dtype=jnp.int32)
    state = jax.ShapeDtypeStruct((heads, HD, HD), bf16)
    tokens = jax.ShapeDtypeStruct((n, cols), bf16)
    tokens32 = jax.ShapeDtypeStruct((n, cols), f32)
    square = 2 * heads * n * n * HD
    narrow = 2 * heads * n * HD * HD

    (tail,) = call(tail_kernel, (state,), narrow, ids, key_in, value_in)
    before = (start_group[:, None] <= group_ids[None, :]) & (group_ids[None, :] < group_ids[:, None])
    carry = spread(tail, before, groups)
    (att_local,) = call(local_kernel, (tokens32,), 2 * square, ids, query_in, key_in, value_in)
    att, sums = call(
        attend_kernel,
        (tokens32, jax.ShapeDtypeStruct((2, n), f32)),
        narrow,
        ids, att_local, query_in, out_grad, gain, carry,
    )
    sums = over_head(sums)
    grad, head_state = call(
        functools.partial(grad_kernel, len(sums)),
        (tokens, state),
        narrow,
        ids, att, query_in, out_grad, gain, *sums,
    )
    after = (start_group[None, :] <= group_ids[:, None]) & (group_ids[:, None] < group_ids[None, :])
    back = spread(head_state, after, groups)
    normed, grad_query, gk, gv = call(
        functools.partial(back_kernel, len(sums)),
        (tokens, tokens, tokens32, tokens32),
        6 * square + narrow,
        ids, att, query_in, key_in, value_in, grad, gain, carry, *sums,
    )
    grad_key, grad_value = call(
        last_kernel, (tokens, tokens), 2 * narrow, ids, key_in, value_in, gk, gv, back
    )
    return normed, grad_query, grad_key, grad_value


def solution(mesh):
    block = P("seq", "head")
    return jax.shard_map(
        local,
        mesh=mesh,
        in_specs=(block, block, block, block, P("head"), P("seq"), P()),
        out_specs=(block, block, block, block),
        check_vma=False,
    )
```

```python
import functools

import jax
import jax.numpy as jnp
from jax import lax
from jax.experimental import pallas as pl
from jax.experimental.pallas import tpu as pltpu
from jax.sharding import PartitionSpec as P

H = 32
HD = 128
WIDTH = H * HD

epsilon = 1e-06

f32 = jnp.float32
bf16 = jnp.bfloat16


def dot(a, b, da, db):
    return lax.dot_general(a, b, (((da,), (db,)), ((), ())), preferred_element_type=f32)


def head_cols(h):
    return slice(h * HD, (h + 1) * HD)


def column(row):
    n = row.shape[1]
    at = lax.broadcasted_iota(jnp.int32, (n, n), 0) == lax.broadcasted_iota(jnp.int32, (n, n), 1)
    return jnp.sum(jnp.where(at, row, 0.0), axis=1, keepdims=True)


def as_row(col):
    n = col.shape[0]
    at = lax.broadcasted_iota(jnp.int32, (n, n), 0) == lax.broadcasted_iota(jnp.int32, (n, n), 1)
    return jnp.sum(jnp.where(at, col, 0.0), axis=0, keepdims=True)


def ids_of(ids_ref):
    row = ids_ref[...].astype(f32)
    return row, column(row)


def first_of(row, col):
    return (col == row[:, :1]).astype(f32)


def last_of(row, col):
    return (col == row[:, -1:]).astype(f32)


def wide(col, dtype=bf16):
    return jnp.broadcast_to(col, (col.shape[0], HD)).astype(dtype)


def tail_kernel(ids_ref, k_ref, v_ref, tail_ref):
    row, col = ids_of(ids_ref)
    last = wide(last_of(row, col))
    for h in range(tail_ref.shape[0]):
        tail_ref[h] = dot(k_ref[:, head_cols(h)] * last, v_ref[:, head_cols(h)], 0, 0).astype(bf16)


def local_kernel(ids_ref, q_ref, k_ref, v_ref, att_ref):
    row, col = ids_of(ids_ref)
    n = row.shape[1]
    t = lax.broadcasted_iota(jnp.int32, (n, n), 0)
    u = lax.broadcasted_iota(jnp.int32, (n, n), 1)
    same = (u <= t) & (col == row)
    for h in range(q_ref.shape[1] // HD):
        c = head_cols(h)
        w = jnp.where(same, dot(q_ref[:, c], k_ref[:, c], 1, 1), 0.0).astype(bf16)
        att_ref[:, c] = dot(w, v_ref[:, c], 1, 0)


def joined(way, start_ref, state_refs, h):
    if way == 0:
        return state_refs[0][h]
    me = lax.axis_index("seq")
    total = None
    for step, ref in enumerate(state_refs, 1):
        if way == 1:
            need = start_ref[me] <= me - step
        else:
            there = me + step
            need = (there < start_ref.shape[0]) & (start_ref[jnp.minimum(there, start_ref.shape[0] - 1)] <= me)
        part = ref[h].astype(f32) * jnp.where(need, 1.0, 0.0)
        total = part if total is None else total + part
    return total.astype(bf16)


def attend_kernel(way, n_states, start_ref, ids_ref, att_ref, q_ref, g_ref, gain_ref, *refs):
    state_refs, (out_ref, sums_ref) = refs[:n_states], refs[n_states:]
    row, col = ids_of(ids_ref)
    first = wide(first_of(row, col))
    square = jnp.zeros((row.shape[1], HD), f32)
    cross = jnp.zeros((row.shape[1], HD), f32)
    for h in range(q_ref.shape[1] // HD):
        c = head_cols(h)
        att = att_ref[:, c] + dot(q_ref[:, c] * first, joined(way, start_ref, state_refs, h), 1, 0)
        out_ref[:, c] = att
        square = square + att * att
        cross = cross + gain_ref[:, c] * g_ref[:, c].astype(f32) * att
    sums_ref[0:1, :] = as_row(jnp.sum(square, axis=1, keepdims=True))
    sums_ref[1:2, :] = as_row(jnp.sum(cross, axis=1, keepdims=True))


def scales(sum_refs):
    total = sum_refs[0][...]
    for ref in sum_refs[1:]:
        total = total + ref[...]
    inverse = lax.rsqrt(total[0:1] / WIDTH + epsilon)
    pull = inverse * inverse * inverse * total[1:2] / WIDTH
    return inverse, pull


def grad_kernel(n_sums, ids_ref, att_ref, q_ref, g_ref, gain_ref, *refs):
    sum_refs, (grad_ref, head_ref) = refs[:n_sums], refs[n_sums:]
    row, col = ids_of(ids_ref)
    first = wide(first_of(row, col))
    inverse, pull = scales(sum_refs)
    inverse, pull = column(inverse), column(pull)
    for h in range(q_ref.shape[1] // HD):
        c = head_cols(h)
        grad = (inverse * gain_ref[:, c] * g_ref[:, c].astype(f32) - pull * att_ref[:, c]).astype(bf16)
        grad_ref[:, c] = grad
        head_ref[h] = dot(q_ref[:, c] * first, grad, 0, 0).astype(bf16)


def back_kernel(way, n_states, n_sums, start_ref, ids_ref, att_ref, q_ref, k_ref, v_ref, grad_ref, gain_ref, *refs):
    state_refs, sum_refs = refs[:n_states], refs[n_states : n_states + n_sums]
    normed_ref, gq_ref, gk_ref, gv_ref = refs[n_states + n_sums :]
    row, col = ids_of(ids_ref)
    first = wide(first_of(row, col))
    n = row.shape[1]
    inverse = column(scales(sum_refs)[0])
    t = lax.broadcasted_iota(jnp.int32, (n, n), 0)
    u = lax.broadcasted_iota(jnp.int32, (n, n), 1)
    same = (u <= t) & (col == row)
    same_t = (t <= u) & (col == row)
    for h in range(q_ref.shape[1] // HD):
        c = head_cols(h)
        q, k, v, grad = q_ref[:, c], k_ref[:, c], v_ref[:, c], grad_ref[:, c]
        normed_ref[:, c] = (att_ref[:, c] * inverse * gain_ref[:, c]).astype(bf16)
        gs = jnp.where(same, dot(grad, v, 1, 1), 0.0).astype(bf16)
        gq_ref[:, c] = (dot(gs, k, 1, 0) + dot(grad * first, joined(way, start_ref, state_refs, h), 1, 1)).astype(bf16)
        gs_t = jnp.where(same_t, dot(v, grad, 1, 1), 0.0).astype(bf16)
        gk_ref[:, c] = dot(gs_t, q, 1, 0)
        w_t = jnp.where(same_t, dot(k, q, 1, 1), 0.0).astype(bf16)
        gv_ref[:, c] = dot(w_t, grad, 1, 0)


def last_kernel(way, n_states, start_ref, ids_ref, k_ref, v_ref, gk_in, gv_in, *refs):
    state_refs, (gk_ref, gv_ref) = refs[:n_states], refs[n_states:]
    row, col = ids_of(ids_ref)
    last = wide(last_of(row, col))
    for h in range(k_ref.shape[1] // HD):
        c = head_cols(h)
        back = joined(-way, start_ref, state_refs, h)
        gk_ref[:, c] = (gk_in[:, c] + dot(v_ref[:, c] * last, back, 1, 1)).astype(bf16)
        gv_ref[:, c] = (gv_in[:, c] + dot(k_ref[:, c] * last, back, 1, 0)).astype(bf16)


def call(kernel, outs, flops, *args):
    moved = sum(a.size * a.dtype.itemsize for a in (*args, *outs))
    vmem = pl.BlockSpec(memory_space=pltpu.VMEM)
    smem = pl.BlockSpec(memory_space=pltpu.SMEM)
    return pl.pallas_call(
        kernel,
        out_shape=outs,
        in_specs=[smem if a.ndim == 1 else vmem for a in args],
        cost_estimate=pl.CostEstimate(flops=flops, bytes_accessed=moved, transcendentals=0),
        compiler_params=pltpu.CompilerParams(vmem_limit_bytes=32 * 2**20),
    )(*args)


def spread(state, mask, groups):
    shape = state.shape
    pieces = state.reshape(groups, -1, shape[-1])
    here = lax.all_to_all(pieces, "seq", 0, 0)
    sums = jnp.einsum("cj,jmn->cmn", mask.astype(bf16), here, preferred_element_type=f32)
    return lax.all_to_all(sums.astype(bf16), "seq", 0, 0).reshape(shape)


def over_head(sums):
    size = lax.axis_size("head")
    power = size & (size - 1) == 0
    return [sums] + [
        lax.ppermute(sums, "head", [(i, i ^ k if power else (i + k) % size) for i in range(size)])
        for k in range(1, size)
    ]


def shifted(state, way, steps):
    groups = lax.axis_size("seq")
    return [
        lax.ppermute(state, "seq", [(i, i + way * k) for i in range(groups) if 0 <= i + way * k < groups])
        for k in range(1, steps + 1)
    ]


def layer(steps, query_in, key_in, value_in, out_grad, gain, ids, start_group):
    n, cols = query_in.shape
    heads = cols // HD
    groups = lax.axis_size("seq")
    way = 1 if steps else 0
    state = jax.ShapeDtypeStruct((heads, HD, HD), bf16)
    tokens = jax.ShapeDtypeStruct((n, cols), bf16)
    tokens32 = jax.ShapeDtypeStruct((n, cols), f32)
    square = 2 * heads * n * n * HD
    narrow = 2 * heads * n * HD * HD
    group_ids = jnp.arange(groups, dtype=jnp.int32)
    before = (start_group[:, None] <= group_ids[None, :]) & (group_ids[None, :] < group_ids[:, None])
    after = (start_group[None, :] <= group_ids[:, None]) & (group_ids[:, None] < group_ids[None, :])

    (tail,) = call(tail_kernel, (state,), narrow, ids, key_in, value_in)
    earlier = shifted(tail, 1, steps) if steps else [spread(tail, before, groups)]
    (att_local,) = call(local_kernel, (tokens32,), 2 * square, ids, query_in, key_in, value_in)
    att, sums = call(
        functools.partial(attend_kernel, way, len(earlier)),
        (tokens32, jax.ShapeDtypeStruct((2, n), f32)),
        narrow,
        start_group, ids, att_local, query_in, out_grad, gain, *earlier,
    )
    sums = over_head(sums)
    grad, head_state = call(
        functools.partial(grad_kernel, len(sums)),
        (tokens, state),
        narrow,
        ids, att, query_in, out_grad, gain, *sums,
    )
    later = shifted(head_state, -1, steps) if steps else [spread(head_state, after, groups)]
    normed, grad_query, gk, gv = call(
        functools.partial(back_kernel, way, len(earlier), len(sums)),
        (tokens, tokens, tokens32, tokens32),
        6 * square + narrow,
        start_group, ids, att, query_in, key_in, value_in, grad, gain, *earlier, *sums,
    )
    grad_key, grad_value = call(
        functools.partial(last_kernel, way, len(later)),
        (tokens, tokens),
        2 * narrow,
        start_group, ids, key_in, value_in, gk, gv, *later,
    )
    return normed, grad_query, grad_key, grad_value


def local(query_in, key_in, value_in, out_grad, norm_gain, doc_ids, start_group):
    n, cols = query_in.shape
    groups = start_group.shape[0]
    reach = jnp.max(jnp.arange(groups, dtype=jnp.int32) - start_group)
    return lax.switch(
        jnp.clip(reach - 1, 0, 2),
        [functools.partial(layer, steps) for steps in (1, 2, 0)],
        query_in, key_in, value_in, out_grad, norm_gain.reshape(1, cols), doc_ids.reshape(1, n), start_group,
    )


def solution(mesh):
    block = P("seq", "head")
    return jax.shard_map(
        local,
        mesh=mesh,
        in_specs=(block, block, block, block, P("head"), P("seq"), P()),
        out_specs=(block, block, block, block),
        check_vma=False,
    )
```

```python
import functools

import jax
import jax.numpy as jnp
from jax import lax
from jax.experimental import pallas as pl
from jax.experimental.pallas import tpu as pltpu
from jax.sharding import PartitionSpec as P

H = 32
HD = 128
WIDTH = H * HD

epsilon = 1e-06

ONE, TWO, PAIRS, ANY = range(4)

f32 = jnp.float32
bf16 = jnp.bfloat16


def dot(a, b, da, db):
    return lax.dot_general(a, b, (((da,), (db,)), ((), ())), preferred_element_type=f32)


def head_cols(h):
    return slice(h * HD, (h + 1) * HD)


def column(row):
    n = row.shape[1]
    at = lax.broadcasted_iota(jnp.int32, (n, n), 0) == lax.broadcasted_iota(jnp.int32, (n, n), 1)
    return jnp.sum(jnp.where(at, row, 0.0), axis=1, keepdims=True)


def as_row(col):
    n = col.shape[0]
    at = lax.broadcasted_iota(jnp.int32, (n, n), 0) == lax.broadcasted_iota(jnp.int32, (n, n), 1)
    return jnp.sum(jnp.where(at, col, 0.0), axis=0, keepdims=True)


def ids_of(ids_ref):
    row = ids_ref[...].astype(f32)
    return row, column(row)


def wide(col, dtype=bf16):
    return jnp.broadcast_to(col, (col.shape[0], HD)).astype(dtype)


def tail_kernel(
    start_hbm, ids_hbm, k_hbm, v_hbm,
    tail_ref, tail2_ref, first_ref, last_ref, needs_ref, plan_ref,
    start_ref, ids_ref, k_ref, v_ref, sems,
):
    chunks = k_ref.shape[0]
    cols = k_ref.shape[2]
    small = [
        pltpu.make_async_copy(ids_hbm, ids_ref, sems.at[2 * chunks]),
        pltpu.make_async_copy(start_hbm, start_ref, sems.at[2 * chunks + 1]),
    ]
    large = []
    for i in range(chunks):
        at = pl.ds(i * cols, cols)
        large.append((
            pltpu.make_async_copy(k_hbm.at[:, at], k_ref.at[i], sems.at[2 * i]),
            pltpu.make_async_copy(v_hbm.at[:, at], v_ref.at[i], sems.at[2 * i + 1]),
        ))
    for copy in small:
        copy.start()
    for pair in large:
        for copy in pair:
            copy.start()
    for copy in small:
        copy.wait()
    me, top = lax.axis_index("seq"), start_ref.shape[0] - 1
    blocks, pairs = jnp.int32(0), jnp.int32(0)
    for c in range(top + 1):
        begin = start_ref[c]
        blocks = jnp.maximum(blocks, c - begin)
        pairs = jnp.maximum(pairs, c // 2 - (begin >> 1))
    plan_ref[0] = jnp.where(blocks <= 2, jnp.maximum(blocks - 1, 0), jnp.where(pairs <= 1, PAIRS, ANY))
    for step in (1, 2):
        needs_ref[step - 1 : step, :] = jnp.full((1, HD), jnp.where(start_ref[me] <= me - step, 1.0, 0.0), f32)
    need, need2 = [
        (me + step <= top) & (start_ref[jnp.minimum(me + step, top)] <= me) for step in (1, 2)
    ]
    row, col = ids_of(ids_ref)
    first_ref[...] = wide((col == row[:, :1]).astype(f32))
    last = (col == row[:, -1:]).astype(f32)
    last_ref[...] = wide(last)
    last = wide(last * jnp.where(need, 1.0, 0.0))
    for i, pair in enumerate(large):
        for copy in pair:
            copy.wait()
        for j in range(cols // HD):
            state = dot(k_ref[i, :, head_cols(j)] * last, v_ref[i, :, head_cols(j)], 0, 0)
            h = i * (cols // HD) + j
            tail_ref[h] = state.astype(bf16)
            tail2_ref[h] = jnp.where(need2, state, 0.0).astype(bf16)


def local_kernel(ids_ref, first_ref, q_ref, k_ref, v_ref, *refs):
    far_refs, att_ref = refs[:-1], refs[-1]
    row, col = ids_of(ids_ref)
    n = row.shape[1]
    t = lax.broadcasted_iota(jnp.int32, (n, n), 0)
    u = lax.broadcasted_iota(jnp.int32, (n, n), 1)
    same = (u <= t) & (col == row)
    for h in range(q_ref.shape[1] // HD):
        c = head_cols(h)
        w = jnp.where(same, dot(q_ref[:, c], k_ref[:, c], 1, 1), 0.0).astype(bf16)
        att = dot(w, v_ref[:, c], 1, 0)
        for far_ref in far_refs:
            att = att + dot(q_ref[:, c] * first_ref[...], far_ref[h], 1, 0)
        att_ref[:, c] = att


def joined(plan, way, refs, h):
    if plan != PAIRS:
        return refs[0][h] if len(refs) == 1 else refs[0][h] + refs[1][h]
    start_ref, twin_ref, inner_ref, outer_ref = refs
    me, top = lax.axis_index("seq"), start_ref.shape[0] - 1
    pair, odd = me >> 1, me & 1
    if way == 1:
        twin = (odd == 1) & (start_ref[me] < me)
        far = start_ref[me] < 2 * pair
    else:
        twin = (odd == 0) & (start_ref[jnp.minimum(me + 1, top)] <= me)
        beyond = 2 * pair + 2
        far = (beyond <= top) & (start_ref[jnp.minimum(beyond, top)] <= me)
    inner = (pair & 1 == 1) == (way == 1)
    zero = jnp.zeros(twin_ref.shape[1:], bf16)
    from_pair = jnp.where(inner, inner_ref[h], outer_ref[h])
    return jnp.where(twin, twin_ref[h], zero) + jnp.where(far, from_pair, zero)


def pair_kernel(way, start_ref, own_ref, twin_ref, out_ref):
    me, top = lax.axis_index("seq"), start_ref.shape[0] - 1
    pair, odd = me >> 1, me & 1
    if way == 1:
        both = start_ref[jnp.minimum(2 * pair + 2, top)] <= 2 * pair
    else:
        both = start_ref[jnp.minimum(2 * pair + 1, top)] < 2 * pair
    own_near = (odd == 1) == (way == 1)
    zero = jnp.zeros(own_ref.shape[1:], bf16)
    for h in range(own_ref.shape[0]):
        own = jnp.where(own_near | both, own_ref[h], zero)
        twin = jnp.where(both | jnp.logical_not(own_near), twin_ref[h], zero)
        out_ref[h] = own + twin


def attend_kernel(plan, first_ref, att_ref, q_ref, g_ref, gain_ref, *refs):
    state_refs, (out_ref, sums_ref) = refs[:-2], refs[-2:]
    first = first_ref[...]
    square = jnp.zeros(first.shape, f32)
    cross = jnp.zeros(first.shape, f32)
    for h in range(q_ref.shape[1] // HD):
        c = head_cols(h)
        att = att_ref[:, c] + dot(q_ref[:, c] * first, joined(plan, 1, state_refs, h), 1, 0)
        out_ref[:, c] = att
        square = square + att * att
        cross = cross + gain_ref[:, c] * g_ref[:, c].astype(f32) * att
    sums_ref[0:1, :] = as_row(jnp.sum(square, axis=1, keepdims=True))
    sums_ref[1:2, :] = as_row(jnp.sum(cross, axis=1, keepdims=True))


def scales(sum_refs):
    total = sum_refs[0][...]
    for ref in sum_refs[1:]:
        total = total + ref[...]
    inverse = lax.rsqrt(total[0:1] / WIDTH + epsilon)
    pull = inverse * inverse * inverse * total[1:2] / WIDTH
    return inverse, pull


def grad_kernel(n_heads, needs_ref, first_ref, att_ref, q_ref, g_ref, gain_ref, *refs):
    sum_refs, grad_ref, head_refs = refs[: -n_heads - 1], refs[-n_heads - 1], refs[-n_heads:]
    first = first_ref[...]
    needs = [jnp.broadcast_to(needs_ref[i : i + 1, :], (HD, HD)) > 0.5 for i in range(n_heads)]
    inverse, pull = scales(sum_refs)
    inverse, pull = column(inverse), column(pull)
    for h in range(q_ref.shape[1] // HD):
        c = head_cols(h)
        grad = (inverse * gain_ref[:, c] * g_ref[:, c].astype(f32) - pull * att_ref[:, c]).astype(bf16)
        grad_ref[:, c] = grad
        state = dot(q_ref[:, c] * first, grad, 0, 0)
        for ref, need in zip(head_refs, needs):
            ref[h] = jnp.where(need, state, 0.0).astype(bf16)


def back_kernel(plan, n_sums, n_far, ids_ref, first_ref, last_ref, att_ref, q_ref, k_ref, v_ref, grad_ref, gain_ref, *refs):
    sum_refs, refs, (normed_ref, gq_ref, gk_ref, gv_ref) = refs[:n_sums], refs[n_sums:-4], refs[-4:]
    far_refs, state_refs = refs[:n_far], refs[n_far:]
    inverse = column(scales(sum_refs)[0])
    row, col = ids_of(ids_ref)
    first = first_ref[...]
    n = row.shape[1]
    t = lax.broadcasted_iota(jnp.int32, (n, n), 0)
    u = lax.broadcasted_iota(jnp.int32, (n, n), 1)
    same = (u <= t) & (col == row)
    same_t = (t <= u) & (col == row)
    for h in range(q_ref.shape[1] // HD):
        c = head_cols(h)
        q, k, v, grad = q_ref[:, c], k_ref[:, c], v_ref[:, c], grad_ref[:, c]
        normed_ref[:, c] = (att_ref[:, c] * inverse * gain_ref[:, c]).astype(bf16)
        gs = jnp.where(same, dot(grad, v, 1, 1), 0.0).astype(bf16)
        gq_ref[:, c] = (dot(gs, k, 1, 0) + dot(grad * first, joined(plan, 1, state_refs, h), 1, 1)).astype(bf16)
        gs_t = jnp.where(same_t, dot(v, grad, 1, 1), 0.0).astype(bf16)
        gk = dot(gs_t, q, 1, 0)
        w_t = jnp.where(same_t, dot(k, q, 1, 1), 0.0).astype(bf16)
        gv = dot(w_t, grad, 1, 0)
        for far_ref in far_refs:
            gk = gk + dot(v * last_ref[...], far_ref[h], 1, 1)
            gv = gv + dot(k * last_ref[...], far_ref[h], 1, 0)
        gk_ref[:, c] = gk
        gv_ref[:, c] = gv


def last_kernel(plan, last_ref, k_ref, v_ref, gk_in, gv_in, *refs):
    state_refs, (gk_hbm, gv_hbm, gk_ref, gv_ref, sems) = refs[:-5], refs[-5:]
    last = last_ref[...]
    chunks, _, cols = gk_ref.shape
    copies = []
    for i in range(chunks):
        for j in range(cols // HD):
            h = i * (cols // HD) + j
            c = head_cols(h)
            back = joined(plan, -1, state_refs, h)
            gk_ref[i, :, head_cols(j)] = (gk_in[:, c] + dot(v_ref[:, c] * last, back, 1, 1)).astype(bf16)
            gv_ref[i, :, head_cols(j)] = (gv_in[:, c] + dot(k_ref[:, c] * last, back, 1, 0)).astype(bf16)
        at = pl.ds(i * cols, cols)
        copies.append(pltpu.make_async_copy(gk_ref.at[i], gk_hbm.at[:, at], sems.at[2 * i]))
        copies.append(pltpu.make_async_copy(gv_ref.at[i], gv_hbm.at[:, at], sems.at[2 * i + 1]))
        copies[-2].start()
        copies[-1].start()
    for copy in copies:
        copy.wait()


def shape_of(a):
    return jax.ShapeDtypeStruct(a.shape, a.dtype)


def call(kernel, outs, flops, *args, in_space=None, out_space=None, scratch=()):
    moved = sum(a.size * a.dtype.itemsize for a in (*args, *outs))

    def spec(a, space):
        return pl.BlockSpec(memory_space=space or (pltpu.SMEM if len(a.shape) == 1 else pltpu.VMEM))

    return pl.pallas_call(
        kernel,
        out_shape=outs,
        in_specs=[spec(a, in_space) for a in args],
        out_specs=tuple(spec(a, out_space) for a in outs),
        scratch_shapes=scratch,
        cost_estimate=pl.CostEstimate(flops=flops, bytes_accessed=moved, transcendentals=0),
        compiler_params=pltpu.CompilerParams(vmem_limit_bytes=32 * 2**20),
    )(*args)


def spread(state, mask, groups):
    shape = state.shape
    pieces = state.reshape(groups, -1, shape[-1])
    here = lax.all_to_all(pieces, "seq", 0, 0)
    sums = jnp.einsum("cj,jmn->cmn", mask.astype(bf16), here, preferred_element_type=f32)
    return lax.all_to_all(sums.astype(bf16), "seq", 0, 0).reshape(shape)


def over_head(sums):
    size = lax.axis_size("head")
    power = size & (size - 1) == 0
    return [sums] + [
        lax.ppermute(sums, "head", [(i, i ^ k if power else (i + k) % size) for i in range(size)])
        for k in range(1, size)
    ]


def exchange(plan, way, states, start_group):
    groups = lax.axis_size("seq")
    if plan in (ONE, TWO):
        return [
            lax.ppermute(state, "seq", [(i, i + way * k) for i in range(groups) if 0 <= i + way * k < groups])
            for k, state in enumerate(states, 1)
        ]
    (state,) = states
    if plan == PAIRS:
        twin = lax.ppermute(state, "seq", [(i, i ^ 1) for i in range(groups)])
        (both,) = call(functools.partial(pair_kernel, way), (shape_of(state),), 0, start_group, state, twin)
        ends = (0, 1, groups - 2, groups - 1)
        outer = [i ^ 1 if i in ends else ((i - 2) ^ 2) + 2 for i in range(groups)]
        return [
            start_group,
            twin,
            lax.ppermute(both, "seq", [(i, i ^ 2) for i in range(groups)]),
            lax.ppermute(both, "seq", list(enumerate(outer))),
        ]
    ids = jnp.arange(groups, dtype=jnp.int32)
    reach = (start_group[:, None] <= ids[None, :]) & (ids[None, :] < ids[:, None])
    return [spread(state, reach if way == 1 else reach.T, groups)]


def layer(plan, tail, tail2, first, last, needs, query_in, key_in, value_in, out_grad, gain, ids, start_group):
    n, cols = query_in.shape
    heads = cols // HD
    tokens = shape_of(query_in)
    tokens32 = jax.ShapeDtypeStruct((n, cols), f32)
    square = 2 * heads * n * n * HD
    narrow = 2 * heads * n * HD * HD

    earlier = exchange(plan, 1, [tail, tail2] if plan == TWO else [tail], start_group)
    near, far = (earlier[:1], earlier[1:]) if plan == TWO else (earlier, [])
    (att_local,) = call(local_kernel, (tokens32,), 2 * square, ids, first, query_in, key_in, value_in, *far)
    att, sums = call(
        functools.partial(attend_kernel, plan),
        (tokens32, jax.ShapeDtypeStruct((2, n), f32)),
        narrow,
        first, att_local, query_in, out_grad, gain, *near,
    )
    sums = over_head(sums)
    n_heads = 2 if plan == TWO else 1
    grad, *head_states = call(
        functools.partial(grad_kernel, n_heads),
        (tokens, *[shape_of(tail)] * n_heads),
        narrow,
        needs, first, att, query_in, out_grad, gain, *sums,
    )
    later = exchange(plan, -1, head_states, start_group)
    near, far = (later[:1], later[1:]) if plan == TWO else (later, [])
    normed, grad_query, gk, gv = call(
        functools.partial(back_kernel, plan, len(sums), len(far)),
        (tokens, tokens, tokens32, tokens32),
        6 * square + narrow,
        ids, first, last, att, query_in, key_in, value_in, grad, gain, *sums, *far, *earlier,
    )
    chunks = 4 if heads % 4 == 0 else 1
    part = pltpu.VMEM((chunks, n, cols // chunks), bf16)
    grad_key, grad_value = call(
        functools.partial(last_kernel, plan),
        (tokens, tokens),
        2 * narrow,
        last, key_in, value_in, gk, gv, *near,
        out_space=pltpu.HBM,
        scratch=[part, part, pltpu.SemaphoreType.DMA((2 * chunks,))],
    )
    return normed, grad_query, grad_key, grad_value


def local(query_in, key_in, value_in, out_grad, norm_gain, doc_ids, start_group):
    n, cols = query_in.shape
    heads = cols // HD
    ids, gain = doc_ids.reshape(1, n), norm_gain.reshape(1, cols)
    state = jax.ShapeDtypeStruct((heads, HD, HD), bf16)
    mask = jax.ShapeDtypeStruct((n, HD), bf16)
    chunks = 4 if heads % 4 == 0 else 1
    part = pltpu.VMEM((chunks, n, cols // chunks), bf16)
    *held, plan = call(
        tail_kernel,
        (
            state, state, mask, mask,
            jax.ShapeDtypeStruct((2, HD), f32), jax.ShapeDtypeStruct((1,), jnp.int32),
        ),
        2 * heads * n * HD * HD,
        start_group, ids, key_in, value_in,
        in_space=pltpu.HBM,
        scratch=[
            pltpu.SMEM(start_group.shape, jnp.int32),
            pltpu.VMEM((1, n), jnp.int32),
            part, part,
            pltpu.SemaphoreType.DMA((2 * chunks + 2,)),
        ],
    )
    plans = (ONE, TWO, PAIRS if start_group.shape[0] % 4 == 0 else ANY, ANY)
    return lax.switch(
        plan[0],
        [functools.partial(layer, way) for way in plans],
        *held, query_in, key_in, value_in, out_grad, gain, ids, start_group,
    )


def solution(mesh):
    block = P("seq", "head")
    return jax.shard_map(
        local,
        mesh=mesh,
        in_specs=(block, block, block, block, P("head"), P("seq"), P()),
        out_specs=(block, block, block, block),
        check_vma=False,
    )
```

```python
import functools

import jax
import jax.numpy as jnp
from jax import lax
from jax.experimental import pallas as pl
from jax.experimental.pallas import tpu as pltpu
from jax.sharding import PartitionSpec as P

H = 32
HD = 128
WIDTH = H * HD

epsilon = 1e-06

ONE, TWO, PAIRS, ANY = range(4)

f32 = jnp.float32
bf16 = jnp.bfloat16


def dot(a, b, da, db):
    return lax.dot_general(a, b, (((da,), (db,)), ((), ())), preferred_element_type=f32)


def head_cols(h):
    return slice(h * HD, (h + 1) * HD)


def column(row):
    n = row.shape[1]
    at = lax.broadcasted_iota(jnp.int32, (n, n), 0) == lax.broadcasted_iota(jnp.int32, (n, n), 1)
    return jnp.sum(jnp.where(at, row, 0.0), axis=1, keepdims=True)


def as_row(col):
    n = col.shape[0]
    at = lax.broadcasted_iota(jnp.int32, (n, n), 0) == lax.broadcasted_iota(jnp.int32, (n, n), 1)
    return jnp.sum(jnp.where(at, col, 0.0), axis=0, keepdims=True)


def ids_of(ids_ref):
    row = ids_ref[...].astype(f32)
    return row, column(row)


def wide(col, dtype=bf16):
    return jnp.broadcast_to(col, (col.shape[0], HD)).astype(dtype)


def tail_kernel(
    start_hbm, ids_hbm, k_hbm, v_hbm, gain_hbm,
    tail_ref, tail2_ref, first_ref, last_ref, needs_ref, ids_ref, gain_ref, k_ref, v_ref, plan_ref,
    start_ref, sems,
):
    pairs = (start_hbm, start_ref), (ids_hbm, ids_ref), (k_hbm, k_ref), (v_hbm, v_ref), (gain_hbm, gain_ref)
    copies = [pltpu.make_async_copy(*pair, sems.at[i]) for i, pair in enumerate(pairs)]
    for copy in copies:
        copy.start()
    for copy in copies[:2]:
        copy.wait()
    me, top = lax.axis_index("seq"), start_ref.shape[0] - 1
    blocks, pairs = jnp.int32(0), jnp.int32(0)
    for c in range(top + 1):
        begin = start_ref[c]
        plan_ref[1 + c] = begin
        blocks = jnp.maximum(blocks, c - begin)
        pairs = jnp.maximum(pairs, c // 2 - (begin >> 1))
    plan_ref[0] = jnp.where(blocks <= 2, jnp.maximum(blocks - 1, 0), jnp.where(pairs <= 1, PAIRS, ANY))
    for step in (1, 2):
        needs_ref[step - 1 : step, :] = jnp.full((1, HD), jnp.where(start_ref[me] <= me - step, 1.0, 0.0), f32)
    need, need2 = [
        (me + step <= top) & (start_ref[jnp.minimum(me + step, top)] <= me) for step in (1, 2)
    ]
    row, col = ids_of(ids_ref)
    first_ref[...] = wide((col == row[:, :1]).astype(f32))
    last = (col == row[:, -1:]).astype(f32)
    last_ref[...] = wide(last)
    last = wide(last * jnp.where(need, 1.0, 0.0))
    for copy in copies[2:]:
        copy.wait()
    for h in range(tail_ref.shape[0]):
        state = dot(k_ref[:, head_cols(h)] * last, v_ref[:, head_cols(h)], 0, 0)
        tail_ref[h] = state.astype(bf16)
        tail2_ref[h] = jnp.where(need2, state, 0.0).astype(bf16)


def local_kernel(q_hbm, g_hbm, ids_ref, k_ref, v_ref, att_ref, q_ref, g_ref, sems):
    copies = [pltpu.make_async_copy(*pair, sems.at[i]) for i, pair in enumerate(((q_hbm, q_ref), (g_hbm, g_ref)))]
    for copy in copies:
        copy.start()
    row, col = ids_of(ids_ref)
    n = row.shape[1]
    t = lax.broadcasted_iota(jnp.int32, (n, n), 0)
    u = lax.broadcasted_iota(jnp.int32, (n, n), 1)
    same = (u <= t) & (col == row)
    for copy in copies:
        copy.wait()
    for h in range(q_ref.shape[1] // HD):
        c = head_cols(h)
        w = jnp.where(same, dot(q_ref[:, c], k_ref[:, c], 1, 1), 0.0).astype(bf16)
        att_ref[:, c] = dot(w, v_ref[:, c], 1, 0)


def joined(plan, way, refs, h):
    if plan != PAIRS:
        return refs[0][h] if len(refs) == 1 else refs[0][h] + refs[1][h]
    start_ref, twin_ref, inner_ref, outer_ref = refs
    me, top = lax.axis_index("seq"), start_ref.shape[0] - 1
    pair, odd = me >> 1, me & 1
    if way == 1:
        twin = (odd == 1) & (start_ref[me] < me)
        far = start_ref[me] < 2 * pair
    else:
        twin = (odd == 0) & (start_ref[jnp.minimum(me + 1, top)] <= me)
        beyond = 2 * pair + 2
        far = (beyond <= top) & (start_ref[jnp.minimum(beyond, top)] <= me)
    inner = (pair & 1 == 1) == (way == 1)
    zero = jnp.zeros(twin_ref.shape[1:], bf16)
    from_pair = jnp.where(inner, inner_ref[h], outer_ref[h])
    return jnp.where(twin, twin_ref[h], zero) + jnp.where(far, from_pair, zero)


def pair_kernel(way, start_ref, own_ref, twin_ref, out_ref):
    me, top = lax.axis_index("seq"), start_ref.shape[0] - 1
    pair, odd = me >> 1, me & 1
    if way == 1:
        both = start_ref[jnp.minimum(2 * pair + 2, top)] <= 2 * pair
    else:
        both = start_ref[jnp.minimum(2 * pair + 1, top)] < 2 * pair
    own_near = (odd == 1) == (way == 1)
    zero = jnp.zeros(own_ref.shape[1:], bf16)
    for h in range(own_ref.shape[0]):
        own = jnp.where(own_near | both, own_ref[h], zero)
        twin = jnp.where(both | jnp.logical_not(own_near), twin_ref[h], zero)
        out_ref[h] = own + twin


def attend_kernel(plan, first_ref, att_ref, q_ref, g_ref, gain_ref, *refs):
    state_refs, (out_ref, sums_ref) = refs[:-2], refs[-2:]
    first = first_ref[...]
    square = jnp.zeros(first.shape, f32)
    cross = jnp.zeros(first.shape, f32)
    for h in range(q_ref.shape[1] // HD):
        c = head_cols(h)
        att = att_ref[:, c] + dot(q_ref[:, c] * first, joined(plan, 1, state_refs, h), 1, 0)
        out_ref[:, c] = att
        square = square + att * att
        cross = cross + gain_ref[:, c] * g_ref[:, c].astype(f32) * att
    sums_ref[0:1, :] = as_row(jnp.sum(square, axis=1, keepdims=True))
    sums_ref[1:2, :] = as_row(jnp.sum(cross, axis=1, keepdims=True))


def scales(sum_refs):
    total = sum_refs[0][...]
    for ref in sum_refs[1:]:
        total = total + ref[...]
    inverse = lax.rsqrt(total[0:1] / WIDTH + epsilon)
    pull = inverse * inverse * inverse * total[1:2] / WIDTH
    return inverse, pull


def grad_kernel(n_heads, needs_ref, first_ref, att_ref, q_ref, g_ref, gain_ref, *refs):
    sum_refs, grad_ref, head_refs = refs[: -n_heads - 1], refs[-n_heads - 1], refs[-n_heads:]
    first = first_ref[...]
    needs = [jnp.broadcast_to(needs_ref[i : i + 1, :], (HD, HD)) > 0.5 for i in range(n_heads)]
    inverse, pull = scales(sum_refs)
    inverse, pull = column(inverse), column(pull)
    for h in range(q_ref.shape[1] // HD):
        c = head_cols(h)
        grad = (inverse * gain_ref[:, c] * g_ref[:, c].astype(f32) - pull * att_ref[:, c]).astype(bf16)
        grad_ref[:, c] = grad
        state = dot(q_ref[:, c] * first, grad, 0, 0)
        for ref, need in zip(head_refs, needs):
            ref[h] = jnp.where(need, state, 0.0).astype(bf16)


def back_kernel(plan, n_sums, ids_ref, first_ref, att_ref, q_ref, k_ref, v_ref, grad_ref, gain_ref, *refs):
    sum_refs, state_refs, (normed_ref, gq_ref, gk_ref, gv_ref) = refs[:n_sums], refs[n_sums:-4], refs[-4:]
    inverse = column(scales(sum_refs)[0])
    row, col = ids_of(ids_ref)
    first = first_ref[...]
    n = row.shape[1]
    t = lax.broadcasted_iota(jnp.int32, (n, n), 0)
    u = lax.broadcasted_iota(jnp.int32, (n, n), 1)
    same = (u <= t) & (col == row)
    same_t = (t <= u) & (col == row)
    for h in range(q_ref.shape[1] // HD):
        c = head_cols(h)
        q, k, v, grad = q_ref[:, c], k_ref[:, c], v_ref[:, c], grad_ref[:, c]
        normed_ref[:, c] = (att_ref[:, c] * inverse * gain_ref[:, c]).astype(bf16)
        gs = jnp.where(same, dot(grad, v, 1, 1), 0.0).astype(bf16)
        gq_ref[:, c] = (dot(gs, k, 1, 0) + dot(grad * first, joined(plan, 1, state_refs, h), 1, 1)).astype(bf16)
        gs_t = jnp.where(same_t, dot(v, grad, 1, 1), 0.0).astype(bf16)
        gk_ref[:, c] = dot(gs_t, q, 1, 0)
        w_t = jnp.where(same_t, dot(k, q, 1, 1), 0.0).astype(bf16)
        gv_ref[:, c] = dot(w_t, grad, 1, 0)


def add_kernel(last_ref, k_ref, v_ref, state_ref, gk_in, gv_in, gk_ref, gv_ref):
    last = last_ref[...]
    for h in range(k_ref.shape[1] // HD):
        c = head_cols(h)
        gk_ref[:, c] = gk_in[:, c] + dot(v_ref[:, c] * last, state_ref[h], 1, 1)
        gv_ref[:, c] = gv_in[:, c] + dot(k_ref[:, c] * last, state_ref[h], 1, 0)


def last_kernel(plan, last_ref, k_ref, v_ref, gk_in, gv_in, *refs):
    state_refs, (gk_hbm, gv_hbm, gk_ref, gv_ref, sems) = refs[:-5], refs[-5:]
    last = last_ref[...]
    chunks, _, cols = gk_ref.shape
    copies = []
    for i in range(chunks):
        for j in range(cols // HD):
            h = i * (cols // HD) + j
            c = head_cols(h)
            back = joined(plan, -1, state_refs, h)
            gk_ref[i, :, head_cols(j)] = (gk_in[:, c] + dot(v_ref[:, c] * last, back, 1, 1)).astype(bf16)
            gv_ref[i, :, head_cols(j)] = (gv_in[:, c] + dot(k_ref[:, c] * last, back, 1, 0)).astype(bf16)
        at = pl.ds(i * cols, cols)
        copies.append(pltpu.make_async_copy(gk_ref.at[i], gk_hbm.at[:, at], sems.at[2 * i]))
        copies.append(pltpu.make_async_copy(gv_ref.at[i], gv_hbm.at[:, at], sems.at[2 * i + 1]))
        copies[-2].start()
        copies[-1].start()
    for copy in copies:
        copy.wait()


def shape_of(a):
    return jax.ShapeDtypeStruct(a.shape, a.dtype)


def in_hbm(a):
    return pltpu.with_memory_space_constraint(a, pltpu.HBM)


def call(kernel, outs, flops, *args, in_space=None, out_space=None, scratch=()):
    moved = sum(a.size * a.dtype.itemsize for a in (*args, *outs))

    def spec(a, space):
        return pl.BlockSpec(memory_space=space or (pltpu.SMEM if len(a.shape) == 1 else pltpu.VMEM))

    return pl.pallas_call(
        kernel,
        out_shape=outs,
        in_specs=[spec(a, space) for a, space in zip(args, in_space or [None] * len(args))],
        out_specs=tuple(spec(a, out_space) for a in outs),
        scratch_shapes=scratch,
        cost_estimate=pl.CostEstimate(flops=flops, bytes_accessed=moved, transcendentals=0),
        compiler_params=pltpu.CompilerParams(vmem_limit_bytes=32 * 2**20),
    )(*args)


def spread(state, mask, groups):
    shape = state.shape
    pieces = state.reshape(groups, -1, shape[-1])
    here = lax.all_to_all(pieces, "seq", 0, 0)
    sums = jnp.einsum("cj,jmn->cmn", mask.astype(bf16), here, preferred_element_type=f32)
    return lax.all_to_all(sums.astype(bf16), "seq", 0, 0).reshape(shape)


def over_head(sums):
    size = lax.axis_size("head")
    power = size & (size - 1) == 0
    return [sums] + [
        lax.ppermute(sums, "head", [(i, i ^ k if power else (i + k) % size) for i in range(size)])
        for k in range(1, size)
    ]


def exchange(plan, way, states, start_group):
    groups = lax.axis_size("seq")
    if plan in (ONE, TWO):
        return [
            lax.ppermute(state, "seq", [(i, i + way * k) for i in range(groups) if 0 <= i + way * k < groups])
            for k, state in enumerate(states, 1)
        ]
    (state,) = states
    if plan == PAIRS:
        twin = lax.ppermute(state, "seq", [(i, i ^ 1) for i in range(groups)])
        (both,) = call(functools.partial(pair_kernel, way), (shape_of(state),), 0, start_group, state, twin)
        ends = (0, 1, groups - 2, groups - 1)
        outer = [i ^ 1 if i in ends else ((i - 2) ^ 2) + 2 for i in range(groups)]
        return [
            start_group,
            twin,
            lax.ppermute(both, "seq", [(i, i ^ 2) for i in range(groups)]),
            lax.ppermute(both, "seq", list(enumerate(outer))),
        ]
    ids = jnp.arange(groups, dtype=jnp.int32)
    reach = (start_group[:, None] <= ids[None, :]) & (ids[None, :] < ids[:, None])
    return [spread(state, reach if way == 1 else reach.T, groups)]


def layer(plan, tail, tail2, first, last, needs, ids, gain, key_in, value_in, plan_and_start, query_in, out_grad):
    n, cols = query_in.shape
    heads = cols // HD
    tokens = shape_of(query_in)
    tokens32 = jax.ShapeDtypeStruct((n, cols), f32)
    square = 2 * heads * n * n * HD
    narrow = 2 * heads * n * HD * HD

    start_group = plan_and_start[1:]
    earlier = exchange(plan, 1, [tail, tail2] if plan == TWO else [tail], start_group)
    att_local, query_in, out_grad = call(
        local_kernel,
        (tokens32, tokens, tokens),
        2 * square,
        in_hbm(query_in), in_hbm(out_grad), ids, key_in, value_in,
        in_space=[pltpu.HBM] * 2 + [pltpu.VMEM] * 3,
        scratch=[pltpu.SemaphoreType.DMA((2,))],
    )
    att, sums = call(
        functools.partial(attend_kernel, plan),
        (tokens32, jax.ShapeDtypeStruct((2, n), f32)),
        narrow,
        first, att_local, query_in, out_grad, gain, *earlier,
    )
    sums = over_head(sums)
    n_heads = 2 if plan == TWO else 1
    grad, *head_states = call(
        functools.partial(grad_kernel, n_heads),
        (tokens, *[shape_of(tail)] * n_heads),
        narrow,
        needs, first, att, query_in, out_grad, gain, *sums,
    )
    later = exchange(plan, -1, head_states, start_group)
    normed, grad_query, gk, gv = call(
        functools.partial(back_kernel, plan, len(sums)),
        (tokens, tokens, tokens32, tokens32),
        6 * square + narrow,
        ids, first, att, query_in, key_in, value_in, grad, gain, *sums, *earlier,
    )
    chunks = 4 if heads % 4 == 0 else 1
    part = pltpu.VMEM((chunks, n, cols // chunks), bf16)
    if plan == TWO:
        near, far = later
        gk, gv = call(add_kernel, (tokens32, tokens32), 2 * narrow, last, key_in, value_in, far, gk, gv)
        later = [near]
    grad_key, grad_value = call(
        functools.partial(last_kernel, plan),
        (tokens, tokens),
        2 * narrow,
        last, key_in, value_in, gk, gv, *later,
        out_space=pltpu.HBM,
        scratch=[part, part, pltpu.SemaphoreType.DMA((2 * chunks,))],
    )
    return normed, grad_query, grad_key, grad_value


def local(query_in, key_in, value_in, out_grad, norm_gain, doc_ids, start_group):
    n, cols = query_in.shape
    heads = cols // HD
    ids, gain = doc_ids.reshape(1, n), norm_gain.reshape(1, cols)
    state = jax.ShapeDtypeStruct((heads, HD, HD), bf16)
    mask = jax.ShapeDtypeStruct((n, HD), bf16)
    *held, plan = call(
        tail_kernel,
        (
            state, state, mask, mask,
            jax.ShapeDtypeStruct((2, HD), f32), shape_of(ids), shape_of(gain), shape_of(key_in), shape_of(value_in),
            jax.ShapeDtypeStruct((1 + start_group.shape[0],), jnp.int32),
        ),
        2 * heads * n * HD * HD,
        *map(in_hbm, (start_group, ids, key_in, value_in, gain)),
        in_space=[pltpu.HBM] * 5,
        scratch=[pltpu.SMEM(start_group.shape, jnp.int32), pltpu.SemaphoreType.DMA((5,))],
    )
    plans = (ONE, TWO, PAIRS if start_group.shape[0] % 4 == 0 else ANY, ANY)
    return lax.switch(
        plan[0],
        [functools.partial(layer, way) for way in plans],
        *held, plan, query_in, out_grad,
    )


def solution(mesh):
    block = P("seq", "head")
    return jax.shard_map(
        local,
        mesh=mesh,
        in_specs=(block, block, block, block, P("head"), P("seq"), P()),
        out_specs=(block, block, block, block),
        check_vma=False,
    )
```

```python
import functools

import jax
import jax.numpy as jnp
from jax import lax
from jax.experimental import pallas as pl
from jax.experimental.pallas import tpu as pltpu
from jax.sharding import PartitionSpec as P

H = 32
HD = 128
WIDTH = H * HD

epsilon = 1e-06

ONE, TWO, PAIRS, ANY = range(4)

f32 = jnp.float32
bf16 = jnp.bfloat16


def dot(a, b, da, db):
    return lax.dot_general(a, b, (((da,), (db,)), ((), ())), preferred_element_type=f32)


def head_cols(h):
    return slice(h * HD, (h + 1) * HD)


def column(row):
    n = row.shape[1]
    at = lax.broadcasted_iota(jnp.int32, (n, n), 0) == lax.broadcasted_iota(jnp.int32, (n, n), 1)
    return jnp.sum(jnp.where(at, row, 0.0), axis=1, keepdims=True)


def as_row(col):
    n = col.shape[0]
    at = lax.broadcasted_iota(jnp.int32, (n, n), 0) == lax.broadcasted_iota(jnp.int32, (n, n), 1)
    return jnp.sum(jnp.where(at, col, 0.0), axis=0, keepdims=True)


def ids_of(ids_ref):
    row = ids_ref[...].astype(f32)
    return row, column(row)


def wide(col, dtype=bf16):
    return jnp.broadcast_to(col, (col.shape[0], HD)).astype(dtype)


BACKWARD, PAIR = 2, 5


def backward_needs(start_ref, me):
    return [start_ref[me] <= me - step for step in (1, 2)]


def pair_needs(start_ref, me, way):
    top = start_ref.shape[0] - 1
    pair, odd = me >> 1, me & 1
    if way == 1:
        both = start_ref[jnp.minimum(2 * pair + 2, top)] <= 2 * pair
        twin = (odd == 1) & (start_ref[me] < me)
        far = start_ref[me] < 2 * pair
    else:
        both = start_ref[jnp.minimum(2 * pair + 1, top)] < 2 * pair
        twin = (odd == 0) & (start_ref[jnp.minimum(me + 1, top)] <= me)
        beyond = jnp.minimum(2 * pair + 2, top)
        far = (2 * pair + 2 <= top) & (start_ref[beyond] <= me)
    near = (odd == 1) == (way == 1)
    inner = (pair & 1 == 1) == (way == 1)
    return [near | both, both | jnp.logical_not(near), twin, far & inner, far & jnp.logical_not(inner)]


def tail_kernel(
    start_hbm, ids_hbm, k_hbm, v_hbm, gain_hbm,
    one_ref, near_ref, far_ref, first_ref, last_ref, needs_ref, ids_ref, gain_ref, k_ref, v_ref, plan_ref,
    start_ref, sems,
):
    pairs = (start_hbm, start_ref), (ids_hbm, ids_ref), (k_hbm, k_ref), (v_hbm, v_ref), (gain_hbm, gain_ref)
    copies = [pltpu.make_async_copy(*pair, sems.at[i]) for i, pair in enumerate(pairs)]
    for copy in copies:
        copy.start()
    for copy in copies[:2]:
        copy.wait()
    me, top = lax.axis_index("seq"), start_ref.shape[0] - 1
    blocks, pairs = jnp.int32(0), jnp.int32(0)
    for c in range(top + 1):
        begin = start_ref[c]
        plan_ref[1 + c] = begin
        blocks = jnp.maximum(blocks, c - begin)
        pairs = jnp.maximum(pairs, c // 2 - (begin >> 1))
    plan_ref[0] = jnp.where(blocks <= 2, jnp.maximum(blocks - 1, 0), jnp.where(pairs <= 1, PAIRS, ANY))
    for row, need in enumerate(backward_needs(start_ref, me) + pair_needs(start_ref, me, 1) + pair_needs(start_ref, me, -1)):
        needs_ref[row : row + 1, :] = jnp.full((1, HD), jnp.where(need, 1.0, 0.0), f32)
    need, need2 = [
        (me + step <= top) & (start_ref[jnp.minimum(me + step, top)] <= me) for step in (1, 2)
    ]
    row, col = ids_of(ids_ref)
    first_ref[...] = wide((col == row[:, :1]).astype(f32))
    last = (col == row[:, -1:]).astype(f32)
    last_ref[...] = wide(last)
    last = wide(last * jnp.where(need, 1.0, 0.0))
    for copy in copies[2:]:
        copy.wait()
    for h in range(one_ref.shape[0]):
        state = dot(k_ref[:, head_cols(h)] * last, v_ref[:, head_cols(h)], 0, 0)
        one_ref[h] = near_ref[h] = state.astype(bf16)
        far_ref[h] = jnp.where(need2, state, 0.0).astype(bf16)


def state_kernel(mask_ref, a_ref, b_ref, state_ref):
    mask = mask_ref[...]
    for h in range(state_ref.shape[0]):
        c = head_cols(h)
        state_ref[h] = dot(a_ref[:, c] * mask, b_ref[:, c], 0, 0).astype(bf16)


def local_kernel(q_hbm, g_hbm, ids_ref, k_ref, v_ref, att_ref, q_ref, g_ref, sems):
    copies = [pltpu.make_async_copy(*pair, sems.at[i]) for i, pair in enumerate(((q_hbm, q_ref), (g_hbm, g_ref)))]
    for copy in copies:
        copy.start()
    row, col = ids_of(ids_ref)
    n = row.shape[1]
    t = lax.broadcasted_iota(jnp.int32, (n, n), 0)
    u = lax.broadcasted_iota(jnp.int32, (n, n), 1)
    same = (u <= t) & (col == row)
    for copy in copies:
        copy.wait()
    for h in range(q_ref.shape[1] // HD):
        c = head_cols(h)
        w = jnp.where(same, dot(q_ref[:, c], k_ref[:, c], 1, 1), 0.0).astype(bf16)
        att_ref[:, c] = dot(w, v_ref[:, c], 1, 0)


def picked(needs_ref, row):
    return jnp.broadcast_to(needs_ref[row : row + 1, :], (HD, HD)) > 0.5


def chosen(picks, refs, h):
    return sum(jnp.where(pick, ref[h].astype(f32), 0.0) for pick, ref in zip(picks, refs)).astype(bf16)


def joined(plan, way, refs):
    if plan == PAIRS:
        needs_ref, *refs = refs
        first = BACKWARD + (2 if way == 1 else 2 + PAIR)
        picks = [picked(needs_ref, first + i) for i in range(3)]
        return lambda h: chosen(picks, refs, h)
    return lambda h: refs[0][h] if len(refs) == 1 else refs[0][h] + refs[1][h]


def pair_kernel(way, needs_ref, own_ref, twin_ref, out_ref):
    first = BACKWARD + (0 if way == 1 else PAIR)
    picks = [picked(needs_ref, first + i) for i in range(2)]
    for h in range(out_ref.shape[0]):
        out_ref[h] = chosen(picks, (own_ref, twin_ref), h)


def attend_kernel(plan, first_ref, att_ref, q_ref, g_ref, gain_ref, *refs):
    state_refs, (out_ref, sums_ref) = refs[:-2], refs[-2:]
    first = first_ref[...]
    carry = joined(plan, 1, state_refs)
    square = jnp.zeros(first.shape, f32)
    cross = jnp.zeros(first.shape, f32)
    for h in range(q_ref.shape[1] // HD):
        c = head_cols(h)
        att = att_ref[:, c] + dot(q_ref[:, c] * first, carry(h), 1, 0)
        out_ref[:, c] = att
        square = square + att * att
        cross = cross + gain_ref[:, c] * g_ref[:, c].astype(f32) * att
    sums_ref[0:1, :] = as_row(jnp.sum(square, axis=1, keepdims=True))
    sums_ref[1:2, :] = as_row(jnp.sum(cross, axis=1, keepdims=True))


def scales(sum_refs):
    total = sum_refs[0][...]
    for ref in sum_refs[1:]:
        total = total + ref[...]
    inverse = lax.rsqrt(total[0:1] / WIDTH + epsilon)
    pull = inverse * inverse * inverse * total[1:2] / WIDTH
    return inverse, pull


def grad_kernel(n_heads, needs_ref, first_ref, att_ref, q_ref, g_ref, gain_ref, *refs):
    sum_refs, grad_ref, head_refs = refs[: -n_heads - 1], refs[-n_heads - 1], refs[-n_heads:]
    first = first_ref[...]
    needs = [picked(needs_ref, i) for i in range(n_heads)]
    inverse, pull = scales(sum_refs)
    inverse, pull = column(inverse), column(pull)
    for h in range(q_ref.shape[1] // HD):
        c = head_cols(h)
        grad = (inverse * gain_ref[:, c] * g_ref[:, c].astype(f32) - pull * att_ref[:, c]).astype(bf16)
        grad_ref[:, c] = grad
        state = dot(q_ref[:, c] * first, grad, 0, 0)
        for ref, need in zip(head_refs, needs):
            ref[h] = jnp.where(need, state, 0.0).astype(bf16)


def back_kernel(plan, n_sums, ids_ref, first_ref, att_ref, q_ref, k_ref, v_ref, grad_ref, gain_ref, *refs):
    sum_refs, state_refs, (normed_ref, gq_ref, gk_ref, gv_ref) = refs[:n_sums], refs[n_sums:-4], refs[-4:]
    inverse = column(scales(sum_refs)[0])
    carry = joined(plan, 1, state_refs)
    row, col = ids_of(ids_ref)
    first = first_ref[...]
    n = row.shape[1]
    t = lax.broadcasted_iota(jnp.int32, (n, n), 0)
    u = lax.broadcasted_iota(jnp.int32, (n, n), 1)
    same = (u <= t) & (col == row)
    same_t = (t <= u) & (col == row)
    for h in range(q_ref.shape[1] // HD):
        c = head_cols(h)
        q, k, v, grad = q_ref[:, c], k_ref[:, c], v_ref[:, c], grad_ref[:, c]
        normed_ref[:, c] = (att_ref[:, c] * inverse * gain_ref[:, c]).astype(bf16)
        gs = jnp.where(same, dot(grad, v, 1, 1), 0.0).astype(bf16)
        gq_ref[:, c] = (dot(gs, k, 1, 0) + dot(grad * first, carry(h), 1, 1)).astype(bf16)
        gs_t = jnp.where(same_t, dot(v, grad, 1, 1), 0.0).astype(bf16)
        gk_ref[:, c] = dot(gs_t, q, 1, 0)
        w_t = jnp.where(same_t, dot(k, q, 1, 1), 0.0).astype(bf16)
        gv_ref[:, c] = dot(w_t, grad, 1, 0)


def add_kernel(last_ref, k_ref, v_ref, state_ref, gk_in, gv_in, gk_ref, gv_ref):
    last = last_ref[...]
    for h in range(k_ref.shape[1] // HD):
        c = head_cols(h)
        gk_ref[:, c] = gk_in[:, c] + dot(v_ref[:, c] * last, state_ref[h], 1, 1)
        gv_ref[:, c] = gv_in[:, c] + dot(k_ref[:, c] * last, state_ref[h], 1, 0)


def last_kernel(plan, last_ref, k_ref, v_ref, gk_in, gv_in, *refs):
    state_refs, (gk_hbm, gv_hbm, gk_ref, gv_ref, sems) = refs[:-5], refs[-5:]
    last = last_ref[...]
    back_of = joined(plan, -1, state_refs)
    chunks, _, cols = gk_ref.shape
    copies = []
    for i in range(chunks):
        for j in range(cols // HD):
            h = i * (cols // HD) + j
            c = head_cols(h)
            back = back_of(h)
            gk_ref[i, :, head_cols(j)] = (gk_in[:, c] + dot(v_ref[:, c] * last, back, 1, 1)).astype(bf16)
            gv_ref[i, :, head_cols(j)] = (gv_in[:, c] + dot(k_ref[:, c] * last, back, 1, 0)).astype(bf16)
        at = pl.ds(i * cols, cols)
        copies.append(pltpu.make_async_copy(gk_ref.at[i], gk_hbm.at[:, at], sems.at[2 * i]))
        copies.append(pltpu.make_async_copy(gv_ref.at[i], gv_hbm.at[:, at], sems.at[2 * i + 1]))
        copies[-2].start()
        copies[-1].start()
    for copy in copies:
        copy.wait()


def shape_of(a):
    return jax.ShapeDtypeStruct(a.shape, a.dtype)


def in_hbm(a):
    return pltpu.with_memory_space_constraint(a, pltpu.HBM)


def call(kernel, outs, flops, *args, in_space=None, out_space=None, scratch=()):
    moved = sum(a.size * a.dtype.itemsize for a in (*args, *outs))

    def spec(a, space):
        return pl.BlockSpec(memory_space=space or (pltpu.SMEM if len(a.shape) == 1 else pltpu.VMEM))

    return pl.pallas_call(
        kernel,
        out_shape=outs,
        in_specs=[spec(a, space) for a, space in zip(args, in_space or [None] * len(args))],
        out_specs=tuple(spec(a, out_space) for a in outs),
        scratch_shapes=scratch,
        cost_estimate=pl.CostEstimate(flops=flops, bytes_accessed=moved, transcendentals=0),
        compiler_params=pltpu.CompilerParams(vmem_limit_bytes=32 * 2**20),
    )(*args)


def spread(state, mask, groups):
    shape = state.shape
    pieces = state.reshape(groups, -1, shape[-1])
    here = lax.all_to_all(pieces, "seq", 0, 0)
    sums = jnp.einsum("cj,jmn->cmn", mask.astype(bf16), here, preferred_element_type=f32)
    return lax.all_to_all(sums.astype(bf16), "seq", 0, 0).reshape(shape)


def over_head(sums):
    size = lax.axis_size("head")
    power = size & (size - 1) == 0
    return [sums] + [
        lax.ppermute(sums, "head", [(i, i ^ k if power else (i + k) % size) for i in range(size)])
        for k in range(1, size)
    ]


def exchange(plan, way, states, needs, plan_and_start):
    groups = lax.axis_size("seq")
    if plan in (ONE, TWO):
        return [
            lax.ppermute(state, "seq", [(i, i + way * k) for i in range(groups) if 0 <= i + way * k < groups])
            for k, state in enumerate(states, 1)
        ]
    (state,) = states
    if plan == PAIRS:
        twin = lax.ppermute(state, "seq", [(i, i ^ 1) for i in range(groups)])
        (both,) = call(functools.partial(pair_kernel, way), (shape_of(state),), 0, needs, state, twin)
        ends = (0, 1, groups - 2, groups - 1)
        outer = [i ^ 1 if i in ends else ((i - 2) ^ 2) + 2 for i in range(groups)]
        return [
            needs,
            twin,
            lax.ppermute(both, "seq", [(i, i ^ 2) for i in range(groups)]),
            lax.ppermute(both, "seq", list(enumerate(outer))),
        ]
    start_group, ids = plan_and_start[1:], jnp.arange(groups, dtype=jnp.int32)
    reach = (start_group[:, None] <= ids[None, :]) & (ids[None, :] < ids[:, None])
    return [spread(state, reach if way == 1 else reach.T, groups)]


def layer(plan, one, near, far, first, last, needs, ids, gain, key_in, value_in, plan_and_start, query_in, out_grad):
    n, cols = query_in.shape
    heads = cols // HD
    tokens = shape_of(query_in)
    tokens32 = jax.ShapeDtypeStruct((n, cols), f32)
    square = 2 * heads * n * n * HD
    narrow = 2 * heads * n * HD * HD

    state = shape_of(one)
    tails = {ONE: [one], TWO: [near, far]}.get(plan) or call(state_kernel, (state,), narrow, last, key_in, value_in)
    earlier = exchange(plan, 1, tails, needs, plan_and_start)
    att_local, query_in, out_grad = call(
        local_kernel,
        (tokens32, tokens, tokens),
        2 * square,
        in_hbm(query_in), in_hbm(out_grad), ids, key_in, value_in,
        in_space=[pltpu.HBM] * 2 + [pltpu.VMEM] * 3,
        scratch=[pltpu.SemaphoreType.DMA((2,))],
    )
    att, sums = call(
        functools.partial(attend_kernel, plan),
        (tokens32, jax.ShapeDtypeStruct((2, n), f32)),
        narrow,
        first, att_local, query_in, out_grad, gain, *earlier,
    )
    sums = over_head(sums)
    n_heads = 2 if plan == TWO else 1
    grad, *head_states = call(
        functools.partial(grad_kernel, n_heads),
        (tokens, *[state] * n_heads),
        narrow,
        needs, first, att, query_in, out_grad, gain, *sums,
    )
    later = exchange(plan, -1, head_states, needs, plan_and_start)
    normed, grad_query, gk, gv = call(
        functools.partial(back_kernel, plan, len(sums)),
        (tokens, tokens, tokens32, tokens32),
        6 * square + narrow,
        ids, first, att, query_in, key_in, value_in, grad, gain, *sums, *earlier,
    )
    chunks = 4 if heads % 4 == 0 else 1
    part = pltpu.VMEM((chunks, n, cols // chunks), bf16)
    if plan == TWO:
        near, far = later
        gk, gv = call(add_kernel, (tokens32, tokens32), 2 * narrow, last, key_in, value_in, far, gk, gv)
        later = [near]
    grad_key, grad_value = call(
        functools.partial(last_kernel, plan),
        (tokens, tokens),
        2 * narrow,
        last, key_in, value_in, gk, gv, *later,
        out_space=pltpu.HBM,
        scratch=[part, part, pltpu.SemaphoreType.DMA((2 * chunks,))],
    )
    return normed, grad_query, grad_key, grad_value


def local(query_in, key_in, value_in, out_grad, norm_gain, doc_ids, start_group):
    n, cols = query_in.shape
    heads = cols // HD
    ids, gain = doc_ids.reshape(1, n), norm_gain.reshape(1, cols)
    state = jax.ShapeDtypeStruct((heads, HD, HD), bf16)
    mask = jax.ShapeDtypeStruct((n, HD), bf16)
    *held, plan = call(
        tail_kernel,
        (
            state, state, state, mask, mask,
            jax.ShapeDtypeStruct((BACKWARD + 2 * PAIR, HD), f32), shape_of(ids), shape_of(gain), shape_of(key_in), shape_of(value_in),
            jax.ShapeDtypeStruct((1 + start_group.shape[0],), jnp.int32),
        ),
        2 * heads * n * HD * HD,
        *map(in_hbm, (start_group, ids, key_in, value_in, gain)),
        in_space=[pltpu.HBM] * 5,
        scratch=[pltpu.SMEM(start_group.shape, jnp.int32), pltpu.SemaphoreType.DMA((5,))],
    )
    plans = (ONE, TWO, PAIRS if start_group.shape[0] % 4 == 0 else ANY, ANY)
    return lax.switch(
        plan[0],
        [functools.partial(layer, way) for way in plans],
        *held, plan, query_in, out_grad,
    )


def solution(mesh):
    block = P("seq", "head")
    return jax.shard_map(
        local,
        mesh=mesh,
        in_specs=(block, block, block, block, P("head"), P("seq"), P()),
        out_specs=(block, block, block, block),
        check_vma=False,
    )
```

```python
import functools

import jax
import jax.numpy as jnp
from jax import lax
from jax.experimental import pallas as pl
from jax.experimental.pallas import tpu as pltpu
from jax.sharding import PartitionSpec as P

H = 32
HD = 128
WIDTH = H * HD

epsilon = 1e-06

ONE, TWO, PAIRS, CHAIN, ANY = range(5)

f32 = jnp.float32
bf16 = jnp.bfloat16


def dot(a, b, da, db):
    return lax.dot_general(a, b, (((da,), (db,)), ((), ())), preferred_element_type=f32)


def head_cols(h):
    return slice(h * HD, (h + 1) * HD)


def column(row):
    n = row.shape[1]
    at = lax.broadcasted_iota(jnp.int32, (n, n), 0) == lax.broadcasted_iota(jnp.int32, (n, n), 1)
    return jnp.sum(jnp.where(at, row, 0.0), axis=1, keepdims=True)


def as_row(col):
    n = col.shape[0]
    at = lax.broadcasted_iota(jnp.int32, (n, n), 0) == lax.broadcasted_iota(jnp.int32, (n, n), 1)
    return jnp.sum(jnp.where(at, col, 0.0), axis=0, keepdims=True)


def ids_of(ids_ref):
    row = ids_ref[...].astype(f32)
    return row, column(row)


def wide(col, dtype=bf16):
    return jnp.broadcast_to(col, (col.shape[0], HD)).astype(dtype)


BACKWARD, PAIR = 2, 7


def backward_needs(start_ref, me):
    return [start_ref[me] <= me - step for step in (1, 2)]


def pair_needs(start_ref, me, way):
    top = start_ref.shape[0] - 1
    pair, odd = me >> 1, me & 1
    if way == 1:
        both = start_ref[jnp.minimum(2 * pair + 2, top)] <= 2 * pair
        twin = (odd == 1) & (start_ref[me] < me)
        far = start_ref[me] < 2 * pair
        through = start_ref[jnp.minimum(2 * pair + 2, top)] < 2 * pair
    else:
        both = start_ref[jnp.minimum(2 * pair + 1, top)] < 2 * pair
        twin = (odd == 0) & (start_ref[jnp.minimum(me + 1, top)] <= me)
        beyond = jnp.minimum(2 * pair + 2, top)
        far = (2 * pair + 2 <= top) & (start_ref[beyond] <= me)
        through = (2 * pair + 2 <= top) & (start_ref[beyond] < 2 * pair)
    near = (odd == 1) == (way == 1)
    inner = (pair & 1 == 1) == (way == 1)
    outer = jnp.logical_not(inner)
    return [
        near | both, both | jnp.logical_not(near),
        twin, far & inner, far & outer,
        through & inner, through & outer,
    ]


def tail_kernel(
    start_hbm, ids_hbm, k_hbm, v_hbm, gain_hbm,
    one_ref, near_ref, far_ref, first_ref, last_ref, needs_ref, ids_ref, gain_ref, k_ref, v_ref, plan_ref,
    start_ref, sems,
):
    pairs = (start_hbm, start_ref), (ids_hbm, ids_ref), (k_hbm, k_ref), (v_hbm, v_ref), (gain_hbm, gain_ref)
    copies = [pltpu.make_async_copy(*pair, sems.at[i]) for i, pair in enumerate(pairs)]
    for copy in copies:
        copy.start()
    for copy in copies[:2]:
        copy.wait()
    me, top = lax.axis_index("seq"), start_ref.shape[0] - 1
    blocks, pairs = jnp.int32(0), jnp.int32(0)
    for c in range(top + 1):
        begin = start_ref[c]
        plan_ref[1 + c] = begin
        blocks = jnp.maximum(blocks, c - begin)
        pairs = jnp.maximum(pairs, c // 2 - (begin >> 1))
    plan_ref[0] = jnp.where(blocks <= 2, jnp.maximum(blocks - 1, 0), jnp.where(pairs <= 2, PAIRS + (pairs - 1), ANY))
    for row, need in enumerate(backward_needs(start_ref, me) + pair_needs(start_ref, me, 1) + pair_needs(start_ref, me, -1)):
        needs_ref[row : row + 1, :] = jnp.full((1, HD), jnp.where(need, 1.0, 0.0), f32)
    need, need2 = [
        (me + step <= top) & (start_ref[jnp.minimum(me + step, top)] <= me) for step in (1, 2)
    ]
    row, col = ids_of(ids_ref)
    first_ref[...] = wide((col == row[:, :1]).astype(f32))
    last = (col == row[:, -1:]).astype(f32)
    last_ref[...] = wide(last)
    last = wide(last * jnp.where(need, 1.0, 0.0))
    for copy in copies[2:]:
        copy.wait()
    for h in range(one_ref.shape[0]):
        state = dot(k_ref[:, head_cols(h)] * last, v_ref[:, head_cols(h)], 0, 0)
        one_ref[h] = near_ref[h] = state.astype(bf16)
        far_ref[h] = jnp.where(need2, state, 0.0).astype(bf16)


def state_kernel(mask_ref, a_ref, b_ref, state_ref):
    mask = mask_ref[...]
    for h in range(state_ref.shape[0]):
        c = head_cols(h)
        state_ref[h] = dot(a_ref[:, c] * mask, b_ref[:, c], 0, 0).astype(bf16)


def local_kernel(q_hbm, g_hbm, ids_ref, k_ref, v_ref, att_ref, q_ref, g_ref, sems):
    copies = [pltpu.make_async_copy(*pair, sems.at[i]) for i, pair in enumerate(((q_hbm, q_ref), (g_hbm, g_ref)))]
    for copy in copies:
        copy.start()
    row, col = ids_of(ids_ref)
    n = row.shape[1]
    t = lax.broadcasted_iota(jnp.int32, (n, n), 0)
    u = lax.broadcasted_iota(jnp.int32, (n, n), 1)
    same = (u <= t) & (col == row)
    for copy in copies:
        copy.wait()
    for h in range(q_ref.shape[1] // HD):
        c = head_cols(h)
        w = jnp.where(same, dot(q_ref[:, c], k_ref[:, c], 1, 1), 0.0).astype(bf16)
        att_ref[:, c] = dot(w, v_ref[:, c], 1, 0)


def picked(needs_ref, row):
    return jnp.broadcast_to(needs_ref[row : row + 1, :], (HD, HD)) > 0.5


def chosen(picks, refs, h):
    return sum(jnp.where(pick, ref[h].astype(f32), 0.0) for pick, ref in zip(picks, refs)).astype(bf16)


def joined(plan, way, refs):
    if plan in (PAIRS, CHAIN):
        needs_ref, *refs = refs
        first = BACKWARD + (2 if way == 1 else 2 + PAIR)
        picks = [picked(needs_ref, first + i) for i in range(3)]
        return lambda h: chosen(picks, refs, h)
    return lambda h: refs[0][h] if len(refs) == 1 else refs[0][h] + refs[1][h]


def pair_kernel(way, needs_ref, own_ref, twin_ref, out_ref):
    first = BACKWARD + (0 if way == 1 else PAIR)
    picks = [picked(needs_ref, first + i) for i in range(2)]
    for h in range(out_ref.shape[0]):
        out_ref[h] = chosen(picks, (own_ref, twin_ref), h)


def chain_kernel(way, needs_ref, own_ref, inner_ref, outer_ref, out_ref):
    first = BACKWARD + (5 if way == 1 else 5 + PAIR)
    picks = [picked(needs_ref, first + i) for i in range(2)]
    for h in range(out_ref.shape[0]):
        out_ref[h] = own_ref[h] + chosen(picks, (inner_ref, outer_ref), h)


def attend_kernel(plan, first_ref, att_ref, q_ref, g_ref, gain_ref, *refs):
    state_refs, (out_ref, sums_ref) = refs[:-2], refs[-2:]
    first = first_ref[...]
    carry = joined(plan, 1, state_refs)
    square = jnp.zeros(first.shape, f32)
    cross = jnp.zeros(first.shape, f32)
    for h in range(q_ref.shape[1] // HD):
        c = head_cols(h)
        att = att_ref[:, c] + dot(q_ref[:, c] * first, carry(h), 1, 0)
        out_ref[:, c] = att
        square = square + att * att
        cross = cross + gain_ref[:, c] * g_ref[:, c].astype(f32) * att
    sums_ref[0:1, :] = as_row(jnp.sum(square, axis=1, keepdims=True))
    sums_ref[1:2, :] = as_row(jnp.sum(cross, axis=1, keepdims=True))


def scales(sum_refs):
    total = sum_refs[0][...]
    for ref in sum_refs[1:]:
        total = total + ref[...]
    inverse = lax.rsqrt(total[0:1] / WIDTH + epsilon)
    pull = inverse * inverse * inverse * total[1:2] / WIDTH
    return inverse, pull


def grad_kernel(n_heads, needs_ref, first_ref, att_ref, q_ref, g_ref, gain_ref, *refs):
    sum_refs, grad_ref, head_refs = refs[: -n_heads - 1], refs[-n_heads - 1], refs[-n_heads:]
    first = first_ref[...]
    needs = [picked(needs_ref, i) for i in range(n_heads)]
    inverse, pull = scales(sum_refs)
    inverse, pull = column(inverse), column(pull)
    for h in range(q_ref.shape[1] // HD):
        c = head_cols(h)
        grad = (inverse * gain_ref[:, c] * g_ref[:, c].astype(f32) - pull * att_ref[:, c]).astype(bf16)
        grad_ref[:, c] = grad
        state = dot(q_ref[:, c] * first, grad, 0, 0)
        for ref, need in zip(head_refs, needs):
            ref[h] = jnp.where(need, state, 0.0).astype(bf16)


def back_kernel(plan, n_sums, ids_ref, first_ref, att_ref, q_ref, k_ref, v_ref, grad_ref, gain_ref, *refs):
    sum_refs, state_refs, (normed_ref, gq_ref, gk_ref, gv_ref) = refs[:n_sums], refs[n_sums:-4], refs[-4:]
    inverse = column(scales(sum_refs)[0])
    carry = joined(plan, 1, state_refs)
    row, col = ids_of(ids_ref)
    first = first_ref[...]
    n = row.shape[1]
    t = lax.broadcasted_iota(jnp.int32, (n, n), 0)
    u = lax.broadcasted_iota(jnp.int32, (n, n), 1)
    same = (u <= t) & (col == row)
    same_t = (t <= u) & (col == row)
    for h in range(q_ref.shape[1] // HD):
        c = head_cols(h)
        q, k, v, grad = q_ref[:, c], k_ref[:, c], v_ref[:, c], grad_ref[:, c]
        normed_ref[:, c] = (att_ref[:, c] * inverse * gain_ref[:, c]).astype(bf16)
        gs = jnp.where(same, dot(grad, v, 1, 1), 0.0).astype(bf16)
        gq_ref[:, c] = (dot(gs, k, 1, 0) + dot(grad * first, carry(h), 1, 1)).astype(bf16)
        gs_t = jnp.where(same_t, dot(v, grad, 1, 1), 0.0).astype(bf16)
        gk_ref[:, c] = dot(gs_t, q, 1, 0)
        w_t = jnp.where(same_t, dot(k, q, 1, 1), 0.0).astype(bf16)
        gv_ref[:, c] = dot(w_t, grad, 1, 0)


def add_kernel(last_ref, k_ref, v_ref, state_ref, gk_in, gv_in, gk_ref, gv_ref):
    last = last_ref[...]
    for h in range(k_ref.shape[1] // HD):
        c = head_cols(h)
        gk_ref[:, c] = gk_in[:, c] + dot(v_ref[:, c] * last, state_ref[h], 1, 1)
        gv_ref[:, c] = gv_in[:, c] + dot(k_ref[:, c] * last, state_ref[h], 1, 0)


def last_kernel(plan, last_ref, k_ref, v_ref, gk_in, gv_in, *refs):
    state_refs, (gk_hbm, gv_hbm, gk_ref, gv_ref, sems) = refs[:-5], refs[-5:]
    last = last_ref[...]
    back_of = joined(plan, -1, state_refs)
    chunks, _, cols = gk_ref.shape
    copies = []
    for i in range(chunks):
        for j in range(cols // HD):
            h = i * (cols // HD) + j
            c = head_cols(h)
            back = back_of(h)
            gk_ref[i, :, head_cols(j)] = (gk_in[:, c] + dot(v_ref[:, c] * last, back, 1, 1)).astype(bf16)
            gv_ref[i, :, head_cols(j)] = (gv_in[:, c] + dot(k_ref[:, c] * last, back, 1, 0)).astype(bf16)
        at = pl.ds(i * cols, cols)
        copies.append(pltpu.make_async_copy(gk_ref.at[i], gk_hbm.at[:, at], sems.at[2 * i]))
        copies.append(pltpu.make_async_copy(gv_ref.at[i], gv_hbm.at[:, at], sems.at[2 * i + 1]))
        copies[-2].start()
        copies[-1].start()
    for copy in copies:
        copy.wait()


def shape_of(a):
    return jax.ShapeDtypeStruct(a.shape, a.dtype)


def in_hbm(a):
    return pltpu.with_memory_space_constraint(a, pltpu.HBM)


def call(kernel, outs, flops, *args, in_space=None, out_space=None, scratch=()):
    moved = sum(a.size * a.dtype.itemsize for a in (*args, *outs))

    def spec(a, space):
        return pl.BlockSpec(memory_space=space or (pltpu.SMEM if len(a.shape) == 1 else pltpu.VMEM))

    return pl.pallas_call(
        kernel,
        out_shape=outs,
        in_specs=[spec(a, space) for a, space in zip(args, in_space or [None] * len(args))],
        out_specs=tuple(spec(a, out_space) for a in outs),
        scratch_shapes=scratch,
        cost_estimate=pl.CostEstimate(flops=flops, bytes_accessed=moved, transcendentals=0),
        compiler_params=pltpu.CompilerParams(vmem_limit_bytes=32 * 2**20),
    )(*args)


def spread(state, mask, groups):
    shape = state.shape
    pieces = state.reshape(groups, -1, shape[-1])
    here = lax.all_to_all(pieces, "seq", 0, 0)
    sums = jnp.einsum("cj,jmn->cmn", mask.astype(bf16), here, preferred_element_type=f32)
    return lax.all_to_all(sums.astype(bf16), "seq", 0, 0).reshape(shape)


def over_head(sums):
    size = lax.axis_size("head")
    power = size & (size - 1) == 0
    return [sums] + [
        lax.ppermute(sums, "head", [(i, i ^ k if power else (i + k) % size) for i in range(size)])
        for k in range(1, size)
    ]


def exchange(plan, way, states, needs, plan_and_start):
    groups = lax.axis_size("seq")
    if plan in (ONE, TWO):
        return [
            lax.ppermute(state, "seq", [(i, i + way * k) for i in range(groups) if 0 <= i + way * k < groups])
            for k, state in enumerate(states, 1)
        ]
    (state,) = states
    if plan in (PAIRS, CHAIN):
        ends = (0, 1, groups - 2, groups - 1)
        inner = [(i, i ^ 2) for i in range(groups)]
        outer = [(i, i ^ 1 if i in ends else ((i - 2) ^ 2) + 2) for i in range(groups)]

        def swapped(pairs):
            return lax.ppermute(given, "seq", pairs)

        twin = lax.ppermute(state, "seq", [(i, i ^ 1) for i in range(groups)])
        (given,) = call(functools.partial(pair_kernel, way), (shape_of(state),), 0, needs, state, twin)
        if plan == CHAIN:
            taken = swapped(inner), swapped(outer)
            (given,) = call(functools.partial(chain_kernel, way), (shape_of(state),), 0, needs, given, *taken)
        return [needs, twin, swapped(inner), swapped(outer)]
    start_group, ids = plan_and_start[1:], jnp.arange(groups, dtype=jnp.int32)
    reach = (start_group[:, None] <= ids[None, :]) & (ids[None, :] < ids[:, None])
    return [spread(state, reach if way == 1 else reach.T, groups)]


def layer(plan, one, near, far, first, last, needs, ids, gain, key_in, value_in, plan_and_start, query_in, out_grad):
    n, cols = query_in.shape
    heads = cols // HD
    tokens = shape_of(query_in)
    tokens32 = jax.ShapeDtypeStruct((n, cols), f32)
    square = 2 * heads * n * n * HD
    narrow = 2 * heads * n * HD * HD

    state = shape_of(one)
    tails = {ONE: [one], TWO: [near, far]}.get(plan) or call(state_kernel, (state,), narrow, last, key_in, value_in)
    earlier = exchange(plan, 1, tails, needs, plan_and_start)
    att_local, query_in, out_grad = call(
        local_kernel,
        (tokens32, tokens, tokens),
        2 * square,
        in_hbm(query_in), in_hbm(out_grad), ids, key_in, value_in,
        in_space=[pltpu.HBM] * 2 + [pltpu.VMEM] * 3,
        scratch=[pltpu.SemaphoreType.DMA((2,))],
    )
    att, sums = call(
        functools.partial(attend_kernel, plan),
        (tokens32, jax.ShapeDtypeStruct((2, n), f32)),
        narrow,
        first, att_local, query_in, out_grad, gain, *earlier,
    )
    sums = over_head(sums)
    n_heads = 2 if plan == TWO else 1
    grad, *head_states = call(
        functools.partial(grad_kernel, n_heads),
        (tokens, *[state] * n_heads),
        narrow,
        needs, first, att, query_in, out_grad, gain, *sums,
    )
    later = exchange(plan, -1, head_states, needs, plan_and_start)
    normed, grad_query, gk, gv = call(
        functools.partial(back_kernel, plan, len(sums)),
        (tokens, tokens, tokens32, tokens32),
        6 * square + narrow,
        ids, first, att, query_in, key_in, value_in, grad, gain, *sums, *earlier,
    )
    chunks = 4 if heads % 4 == 0 else 1
    part = pltpu.VMEM((chunks, n, cols // chunks), bf16)
    if plan == TWO:
        near, far = later
        gk, gv = call(add_kernel, (tokens32, tokens32), 2 * narrow, last, key_in, value_in, far, gk, gv)
        later = [near]
    grad_key, grad_value = call(
        functools.partial(last_kernel, plan),
        (tokens, tokens),
        2 * narrow,
        last, key_in, value_in, gk, gv, *later,
        out_space=pltpu.HBM,
        scratch=[part, part, pltpu.SemaphoreType.DMA((2 * chunks,))],
    )
    return normed, grad_query, grad_key, grad_value


def local(query_in, key_in, value_in, out_grad, norm_gain, doc_ids, start_group):
    n, cols = query_in.shape
    heads = cols // HD
    ids, gain = doc_ids.reshape(1, n), norm_gain.reshape(1, cols)
    state = jax.ShapeDtypeStruct((heads, HD, HD), bf16)
    mask = jax.ShapeDtypeStruct((n, HD), bf16)
    *held, plan = call(
        tail_kernel,
        (
            state, state, state, mask, mask,
            jax.ShapeDtypeStruct((BACKWARD + 2 * PAIR, HD), f32), shape_of(ids), shape_of(gain), shape_of(key_in), shape_of(value_in),
            jax.ShapeDtypeStruct((1 + start_group.shape[0],), jnp.int32),
        ),
        2 * heads * n * HD * HD,
        *map(in_hbm, (start_group, ids, key_in, value_in, gain)),
        in_space=[pltpu.HBM] * 5,
        scratch=[pltpu.SMEM(start_group.shape, jnp.int32), pltpu.SemaphoreType.DMA((5,))],
    )
    by_pairs = (PAIRS, CHAIN) if start_group.shape[0] % 4 == 0 else (ANY, ANY)
    plans = (ONE, TWO, *by_pairs, ANY)
    return lax.switch(
        plan[0],
        [functools.partial(layer, way) for way in plans],
        *held, plan, query_in, out_grad,
    )


def solution(mesh):
    block = P("seq", "head")
    return jax.shard_map(
        local,
        mesh=mesh,
        in_specs=(block, block, block, block, P("head"), P("seq"), P()),
        out_specs=(block, block, block, block),
        check_vma=False,
    )
```

```python
import functools

import jax
import jax.numpy as jnp
from jax import lax
from jax.experimental import pallas as pl
from jax.experimental.pallas import tpu as pltpu
from jax.sharding import PartitionSpec as P

H = 32
HD = 128
WIDTH = H * HD

epsilon = 1e-06

ONE, TWO, PAIRS, CHAIN, ANY = range(5)

f32 = jnp.float32
bf16 = jnp.bfloat16


def dot(a, b, da, db):
    return lax.dot_general(a, b, (((da,), (db,)), ((), ())), preferred_element_type=f32)


def head_cols(h):
    return slice(h * HD, (h + 1) * HD)


def column(row):
    n = row.shape[1]
    at = lax.broadcasted_iota(jnp.int32, (n, n), 0) == lax.broadcasted_iota(jnp.int32, (n, n), 1)
    return jnp.sum(jnp.where(at, row, 0.0), axis=1, keepdims=True)


def as_row(col):
    n = col.shape[0]
    at = lax.broadcasted_iota(jnp.int32, (n, n), 0) == lax.broadcasted_iota(jnp.int32, (n, n), 1)
    return jnp.sum(jnp.where(at, col, 0.0), axis=0, keepdims=True)


def ids_of(ids_ref):
    row = ids_ref[...].astype(f32)
    return row, column(row)


def wide(col, dtype=bf16):
    return jnp.broadcast_to(col, (col.shape[0], HD)).astype(dtype)


BACKWARD, PAIR = 2, 7


def backward_needs(start_ref, me):
    return [start_ref[me] <= me - step for step in (1, 2)]


def pair_needs(start_ref, me, way):
    top = start_ref.shape[0] - 1
    pair, odd = me >> 1, me & 1
    if way == 1:
        both = start_ref[jnp.minimum(2 * pair + 2, top)] <= 2 * pair
        twin = (odd == 1) & (start_ref[me] < me)
        far = start_ref[me] < 2 * pair
        through = start_ref[jnp.minimum(2 * pair + 2, top)] < 2 * pair
    else:
        both = start_ref[jnp.minimum(2 * pair + 1, top)] < 2 * pair
        twin = (odd == 0) & (start_ref[jnp.minimum(me + 1, top)] <= me)
        beyond = jnp.minimum(2 * pair + 2, top)
        far = (2 * pair + 2 <= top) & (start_ref[beyond] <= me)
        through = (2 * pair + 2 <= top) & (start_ref[beyond] < 2 * pair)
    near = (odd == 1) == (way == 1)
    inner = (pair & 1 == 1) == (way == 1)
    outer = jnp.logical_not(inner)
    return [
        near | both, both | jnp.logical_not(near),
        twin, far & inner, far & outer,
        through & inner, through & outer,
    ]


def tail_kernel(
    start_hbm, ids_hbm, k_hbm, v_hbm, gain_hbm,
    one_ref, near_ref, far_ref, first_ref, last_ref, needs_ref, ids_ref, gain_ref, k_ref, v_ref, plan_ref,
    start_ref, sems,
):
    pairs = (start_hbm, start_ref), (ids_hbm, ids_ref), (k_hbm, k_ref), (v_hbm, v_ref), (gain_hbm, gain_ref)
    copies = [pltpu.make_async_copy(*pair, sems.at[i]) for i, pair in enumerate(pairs)]
    for copy in copies:
        copy.start()
    for copy in copies[:2]:
        copy.wait()
    me, top = lax.axis_index("seq"), start_ref.shape[0] - 1
    blocks, pairs = jnp.int32(0), jnp.int32(0)
    for c in range(top + 1):
        begin = start_ref[c]
        plan_ref[1 + c] = begin
        blocks = jnp.maximum(blocks, c - begin)
        pairs = jnp.maximum(pairs, c // 2 - (begin >> 1))
    plan_ref[0] = jnp.where(blocks <= 2, jnp.maximum(blocks - 1, 0), jnp.where(pairs <= 2, PAIRS + (pairs - 1), ANY))
    for row, need in enumerate(backward_needs(start_ref, me) + pair_needs(start_ref, me, 1) + pair_needs(start_ref, me, -1)):
        needs_ref[row : row + 1, :] = jnp.full((1, HD), jnp.where(need, 1.0, 0.0), f32)
    need, need2 = [
        (me + step <= top) & (start_ref[jnp.minimum(me + step, top)] <= me) for step in (1, 2)
    ]
    row, col = ids_of(ids_ref)
    first_ref[...] = wide((col == row[:, :1]).astype(f32))
    last = (col == row[:, -1:]).astype(f32)
    last_ref[...] = wide(last)
    last = wide(last * jnp.where(need, 1.0, 0.0))
    for copy in copies[2:]:
        copy.wait()
    for h in range(one_ref.shape[0]):
        state = dot(k_ref[:, head_cols(h)] * last, v_ref[:, head_cols(h)], 0, 0)
        one_ref[h] = near_ref[h] = state.astype(bf16)
        far_ref[h] = jnp.where(need2, state, 0.0).astype(bf16)


def state_kernel(mask_ref, a_ref, b_ref, state_ref):
    mask = mask_ref[...]
    for h in range(state_ref.shape[0]):
        c = head_cols(h)
        state_ref[h] = dot(a_ref[:, c] * mask, b_ref[:, c], 0, 0).astype(bf16)


def local_kernel(q_hbm, g_hbm, ids_ref, k_ref, v_ref, att_ref, q_ref, g_ref, sems):
    copies = [pltpu.make_async_copy(*pair, sems.at[i]) for i, pair in enumerate(((q_hbm, q_ref), (g_hbm, g_ref)))]
    for copy in copies:
        copy.start()
    row, col = ids_of(ids_ref)
    n = row.shape[1]
    t = lax.broadcasted_iota(jnp.int32, (n, n), 0)
    u = lax.broadcasted_iota(jnp.int32, (n, n), 1)
    same = (u <= t) & (col == row)
    for copy in copies:
        copy.wait()
    for h in range(q_ref.shape[1] // HD):
        c = head_cols(h)
        w = jnp.where(same, dot(q_ref[:, c], k_ref[:, c], 1, 1), 0.0).astype(bf16)
        att_ref[:, c] = dot(w, v_ref[:, c], 1, 0)


def picked(needs_ref, row):
    return jnp.broadcast_to(needs_ref[row : row + 1, :], (HD, HD)) > 0.5


def chosen(picks, refs, h):
    return sum(jnp.where(pick, ref[h].astype(f32), 0.0) for pick, ref in zip(picks, refs)).astype(bf16)


def joined(plan, way, refs):
    if plan in (PAIRS, CHAIN):
        needs_ref, *refs = refs
        first = BACKWARD + (2 if way == 1 else 2 + PAIR)
        picks = [picked(needs_ref, first + i) for i in range(3)]
        return lambda h: chosen(picks, refs, h)
    return lambda h: refs[0][h] if len(refs) == 1 else refs[0][h] + refs[1][h]


def pair_kernel(way, needs_ref, own_ref, twin_ref, out_ref):
    first = BACKWARD + (0 if way == 1 else PAIR)
    picks = [picked(needs_ref, first + i) for i in range(2)]
    for h in range(out_ref.shape[0]):
        out_ref[h] = chosen(picks, (own_ref, twin_ref), h)


def chain_kernel(way, needs_ref, own_ref, inner_ref, outer_ref, out_ref):
    first = BACKWARD + (5 if way == 1 else 5 + PAIR)
    picks = [picked(needs_ref, first + i) for i in range(2)]
    for h in range(out_ref.shape[0]):
        out_ref[h] = own_ref[h] + chosen(picks, (inner_ref, outer_ref), h)


def attend_kernel(plan, first_ref, att_ref, q_ref, g_ref, gain_ref, *refs):
    state_refs, (out_ref, sums_ref) = refs[:-2], refs[-2:]
    first = first_ref[...]
    carry = joined(plan, 1, state_refs)
    square = jnp.zeros(first.shape, f32)
    cross = jnp.zeros(first.shape, f32)
    for h in range(q_ref.shape[1] // HD):
        c = head_cols(h)
        att = att_ref[:, c] + dot(q_ref[:, c] * first, carry(h), 1, 0)
        out_ref[:, c] = att
        square = square + att * att
        cross = cross + gain_ref[:, c] * g_ref[:, c].astype(f32) * att
    sums_ref[0:1, :] = as_row(jnp.sum(square, axis=1, keepdims=True))
    sums_ref[1:2, :] = as_row(jnp.sum(cross, axis=1, keepdims=True))


def scales(sum_refs):
    total = sum_refs[0][...]
    for ref in sum_refs[1:]:
        total = total + ref[...]
    inverse = lax.rsqrt(total[0:1] / WIDTH + epsilon)
    pull = inverse * inverse * inverse * total[1:2] / WIDTH
    return inverse, pull


def grad_kernel(n_heads, needs_ref, first_ref, att_ref, q_ref, g_ref, gain_ref, *refs):
    sum_refs, grad_ref, head_refs = refs[: -n_heads - 1], refs[-n_heads - 1], refs[-n_heads:]
    first = first_ref[...]
    needs = [picked(needs_ref, i) for i in range(n_heads)]
    inverse, pull = scales(sum_refs)
    inverse, pull = column(inverse), column(pull)
    for h in range(q_ref.shape[1] // HD):
        c = head_cols(h)
        grad = (inverse * gain_ref[:, c] * g_ref[:, c].astype(f32) - pull * att_ref[:, c]).astype(bf16)
        grad_ref[:, c] = grad
        state = dot(q_ref[:, c] * first, grad, 0, 0)
        for ref, need in zip(head_refs, needs):
            ref[h] = jnp.where(need, state, 0.0).astype(bf16)


def back_kernel(plan, n_sums, ids_ref, first_ref, att_ref, q_ref, k_ref, v_ref, grad_ref, gain_ref, *refs):
    sum_refs, state_refs, (normed_ref, gq_ref, gk_ref, gv_ref) = refs[:n_sums], refs[n_sums:-4], refs[-4:]
    inverse = column(scales(sum_refs)[0])
    carry = joined(plan, 1, state_refs)
    row, col = ids_of(ids_ref)
    first = first_ref[...]
    n = row.shape[1]
    t = lax.broadcasted_iota(jnp.int32, (n, n), 0)
    u = lax.broadcasted_iota(jnp.int32, (n, n), 1)
    same = (u <= t) & (col == row)
    same_t = (t <= u) & (col == row)
    for h in range(q_ref.shape[1] // HD):
        c = head_cols(h)
        q, k, v, grad = q_ref[:, c], k_ref[:, c], v_ref[:, c], grad_ref[:, c]
        normed_ref[:, c] = (att_ref[:, c] * inverse * gain_ref[:, c]).astype(bf16)
        gs = jnp.where(same, dot(grad, v, 1, 1), 0.0).astype(bf16)
        gq_ref[:, c] = (dot(gs, k, 1, 0) + dot(grad * first, carry(h), 1, 1)).astype(bf16)
        gs_t = jnp.where(same_t, dot(v, grad, 1, 1), 0.0).astype(bf16)
        gk_ref[:, c] = dot(gs_t, q, 1, 0)
        w_t = jnp.where(same_t, dot(k, q, 1, 1), 0.0).astype(bf16)
        gv_ref[:, c] = dot(w_t, grad, 1, 0)


def add_kernel(last_ref, k_ref, v_ref, state_ref, gk_in, gv_in, gk_ref, gv_ref):
    last = last_ref[...]
    for h in range(k_ref.shape[1] // HD):
        c = head_cols(h)
        gk_ref[:, c] = gk_in[:, c] + dot(v_ref[:, c] * last, state_ref[h], 1, 1)
        gv_ref[:, c] = gv_in[:, c] + dot(k_ref[:, c] * last, state_ref[h], 1, 0)


def last_kernel(plan, last_ref, k_ref, v_ref, gk_in, gv_in, *refs):
    state_refs, (gk_hbm, gv_hbm, gk_ref, gv_ref, sems) = refs[:-5], refs[-5:]
    last = last_ref[...]
    back_of = joined(plan, -1, state_refs)
    chunks, _, cols = gk_ref.shape
    copies = []
    for i in range(chunks):
        for j in range(cols // HD):
            h = i * (cols // HD) + j
            c = head_cols(h)
            back = back_of(h)
            gk_ref[i, :, head_cols(j)] = (gk_in[:, c] + dot(v_ref[:, c] * last, back, 1, 1)).astype(bf16)
            gv_ref[i, :, head_cols(j)] = (gv_in[:, c] + dot(k_ref[:, c] * last, back, 1, 0)).astype(bf16)
        at = pl.ds(i * cols, cols)
        copies.append(pltpu.make_async_copy(gk_ref.at[i], gk_hbm.at[:, at], sems.at[2 * i]))
        copies.append(pltpu.make_async_copy(gv_ref.at[i], gv_hbm.at[:, at], sems.at[2 * i + 1]))
        copies[-2].start()
        copies[-1].start()
    for copy in copies:
        copy.wait()


def shape_of(a):
    return jax.ShapeDtypeStruct(a.shape, a.dtype)


def in_hbm(a):
    return pltpu.with_memory_space_constraint(a, pltpu.HBM)


def call(kernel, outs, flops, *args, in_space=None, out_space=None, scratch=()):
    moved = sum(a.size * a.dtype.itemsize for a in (*args, *outs))

    def spec(a, space):
        return pl.BlockSpec(memory_space=space or (pltpu.SMEM if len(a.shape) == 1 else pltpu.VMEM))

    return pl.pallas_call(
        kernel,
        out_shape=outs,
        in_specs=[spec(a, space) for a, space in zip(args, in_space or [None] * len(args))],
        out_specs=tuple(spec(a, out_space) for a in outs),
        scratch_shapes=scratch,
        cost_estimate=pl.CostEstimate(flops=flops, bytes_accessed=moved, transcendentals=0),
        compiler_params=pltpu.CompilerParams(vmem_limit_bytes=32 * 2**20),
    )(*args)


def spread(state, mask, groups):
    shape = state.shape
    pieces = state.reshape(groups, -1, shape[-1])
    here = lax.all_to_all(pieces, "seq", 0, 0)
    sums = jnp.einsum("cj,jmn->cmn", mask.astype(bf16), here, preferred_element_type=f32)
    return lax.all_to_all(sums.astype(bf16), "seq", 0, 0).reshape(shape)


def over_head(sums):
    size = lax.axis_size("head")
    power = size & (size - 1) == 0
    return [sums] + [
        lax.ppermute(sums, "head", [(i, i ^ k if power else (i + k) % size) for i in range(size)])
        for k in range(1, size)
    ]


def exchange(plan, way, states, needs, plan_and_start):
    groups = lax.axis_size("seq")
    if plan in (ONE, TWO):
        return [
            lax.ppermute(state, "seq", [
                (i, (i + way * k) % groups)
                for i in range(groups)
                if 0 <= i + way * k < groups or (plan == TWO and way == 1 and k == 1)
            ])
            for k, state in enumerate(states, 1)
        ]
    (state,) = states
    if plan in (PAIRS, CHAIN):
        ends = (0, 1, groups - 2, groups - 1)
        inner = [(i, i ^ 2) for i in range(groups)]
        outer = [(i, i ^ 1 if i in ends else ((i - 2) ^ 2) + 2) for i in range(groups)]

        def swapped(pairs):
            return lax.ppermute(given, "seq", pairs)

        twin = lax.ppermute(state, "seq", [(i, i ^ 1) for i in range(groups)])
        (given,) = call(functools.partial(pair_kernel, way), (shape_of(state),), 0, needs, state, twin)
        if plan == CHAIN:
            taken = swapped(inner), swapped(outer)
            (given,) = call(functools.partial(chain_kernel, way), (shape_of(state),), 0, needs, given, *taken)
        return [needs, twin, swapped(inner), swapped(outer)]
    start_group, ids = plan_and_start[1:], jnp.arange(groups, dtype=jnp.int32)
    reach = (start_group[:, None] <= ids[None, :]) & (ids[None, :] < ids[:, None])
    return [spread(state, reach if way == 1 else reach.T, groups)]


def layer(plan, one, near, far, first, last, needs, ids, gain, key_in, value_in, plan_and_start, query_in, out_grad):
    n, cols = query_in.shape
    heads = cols // HD
    tokens = shape_of(query_in)
    tokens32 = jax.ShapeDtypeStruct((n, cols), f32)
    square = 2 * heads * n * n * HD
    narrow = 2 * heads * n * HD * HD

    state = shape_of(one)
    tails = {ONE: [one], TWO: [near, far]}.get(plan) or call(state_kernel, (state,), narrow, last, key_in, value_in)
    earlier = exchange(plan, 1, tails, needs, plan_and_start)
    att_local, query_in, out_grad = call(
        local_kernel,
        (tokens32, tokens, tokens),
        2 * square,
        in_hbm(query_in), in_hbm(out_grad), ids, key_in, value_in,
        in_space=[pltpu.HBM] * 2 + [pltpu.VMEM] * 3,
        scratch=[pltpu.SemaphoreType.DMA((2,))],
    )
    att, sums = call(
        functools.partial(attend_kernel, plan),
        (tokens32, jax.ShapeDtypeStruct((2, n), f32)),
        narrow,
        first, att_local, query_in, out_grad, gain, *earlier,
    )
    sums = over_head(sums)
    n_heads = 2 if plan == TWO else 1
    grad, *head_states = call(
        functools.partial(grad_kernel, n_heads),
        (tokens, *[state] * n_heads),
        narrow,
        needs, first, att, query_in, out_grad, gain, *sums,
    )
    later = exchange(plan, -1, head_states, needs, plan_and_start)
    normed, grad_query, gk, gv = call(
        functools.partial(back_kernel, plan, len(sums)),
        (tokens, tokens, tokens32, tokens32),
        6 * square + narrow,
        ids, first, att, query_in, key_in, value_in, grad, gain, *sums, *earlier,
    )
    chunks = 4 if heads % 4 == 0 else 1
    part = pltpu.VMEM((chunks, n, cols // chunks), bf16)
    if plan == TWO:
        near, far = later
        gk, gv = call(add_kernel, (tokens32, tokens32), 2 * narrow, last, key_in, value_in, far, gk, gv)
        later = [near]
    grad_key, grad_value = call(
        functools.partial(last_kernel, plan),
        (tokens, tokens),
        2 * narrow,
        last, key_in, value_in, gk, gv, *later,
        out_space=pltpu.HBM,
        scratch=[part, part, pltpu.SemaphoreType.DMA((2 * chunks,))],
    )
    return normed, grad_query, grad_key, grad_value


def local(query_in, key_in, value_in, out_grad, norm_gain, doc_ids, start_group):
    n, cols = query_in.shape
    heads = cols // HD
    ids, gain = doc_ids.reshape(1, n), norm_gain.reshape(1, cols)
    state = jax.ShapeDtypeStruct((heads, HD, HD), bf16)
    mask = jax.ShapeDtypeStruct((n, HD), bf16)
    *held, plan = call(
        tail_kernel,
        (
            state, state, state, mask, mask,
            jax.ShapeDtypeStruct((BACKWARD + 2 * PAIR, HD), f32), shape_of(ids), shape_of(gain), shape_of(key_in), shape_of(value_in),
            jax.ShapeDtypeStruct((1 + start_group.shape[0],), jnp.int32),
        ),
        2 * heads * n * HD * HD,
        *map(in_hbm, (start_group, ids, key_in, value_in, gain)),
        in_space=[pltpu.HBM] * 5,
        scratch=[pltpu.SMEM(start_group.shape, jnp.int32), pltpu.SemaphoreType.DMA((5,))],
    )
    by_pairs = (PAIRS, CHAIN) if start_group.shape[0] % 4 == 0 else (ANY, ANY)
    plans = (ONE, TWO, *by_pairs, ANY)
    return lax.switch(
        plan[0],
        [functools.partial(layer, way) for way in plans],
        *held, plan, query_in, out_grad,
    )


def solution(mesh):
    block = P("seq", "head")
    return jax.shard_map(
        local,
        mesh=mesh,
        in_specs=(block, block, block, block, P("head"), P("seq"), P()),
        out_specs=(block, block, block, block),
        check_vma=False,
    )
```

```python
import functools

import jax
import jax.numpy as jnp
from jax import lax
from jax.experimental import pallas as pl
from jax.experimental.pallas import tpu as pltpu
from jax.sharding import PartitionSpec as P

H = 32
HD = 128
WIDTH = H * HD

epsilon = 1e-06

ONE, ODD, TWO, PAIRS, CHAIN, ANY = range(6)

f32 = jnp.float32
bf16 = jnp.bfloat16


def dot(a, b, da, db):
    return lax.dot_general(a, b, (((da,), (db,)), ((), ())), preferred_element_type=f32)


def head_cols(h):
    return slice(h * HD, (h + 1) * HD) if isinstance(h, int) else pl.ds(pl.multiple_of(h * HD, HD), HD)


def each_head(plan, heads, body):
    if plan in (PAIRS, CHAIN, ANY):
        pl.loop(0, heads)(body)
    else:
        for h in range(heads):
            body(h)


def column(row):
    n = row.shape[1]
    at = lax.broadcasted_iota(jnp.int32, (n, n), 0) == lax.broadcasted_iota(jnp.int32, (n, n), 1)
    return jnp.sum(jnp.where(at, row, 0.0), axis=1, keepdims=True)


def as_row(col):
    n = col.shape[0]
    at = lax.broadcasted_iota(jnp.int32, (n, n), 0) == lax.broadcasted_iota(jnp.int32, (n, n), 1)
    return jnp.sum(jnp.where(at, col, 0.0), axis=0, keepdims=True)


def ids_of(ids_ref):
    row = ids_ref[...].astype(f32)
    return row, column(row)


def wide(col, dtype=bf16):
    return jnp.broadcast_to(col, (col.shape[0], HD)).astype(dtype)


BACKWARD, PAIR = 2, 7


def backward_needs(start_ref, me):
    return [start_ref[me] <= me - step for step in (1, 2)]


def pair_needs(start_ref, me, way):
    top = start_ref.shape[0] - 1
    pair, odd = me >> 1, me & 1
    if way == 1:
        both = start_ref[jnp.minimum(2 * pair + 2, top)] <= 2 * pair
        twin = (odd == 1) & (start_ref[me] < me)
        far = start_ref[me] < 2 * pair
        through = start_ref[jnp.minimum(2 * pair + 2, top)] < 2 * pair
    else:
        both = start_ref[jnp.minimum(2 * pair + 1, top)] < 2 * pair
        twin = (odd == 0) & (start_ref[jnp.minimum(me + 1, top)] <= me)
        beyond = jnp.minimum(2 * pair + 2, top)
        far = (2 * pair + 2 <= top) & (start_ref[beyond] <= me)
        through = (2 * pair + 2 <= top) & (start_ref[beyond] < 2 * pair)
    near = (odd == 1) == (way == 1)
    inner = (pair & 1 == 1) == (way == 1)
    outer = jnp.logical_not(inner)
    return [
        near | both, both | jnp.logical_not(near),
        twin, far & inner, far & outer,
        through & inner, through & outer,
    ]


def tail_kernel(
    start_hbm, ids_hbm, k_hbm, v_hbm, gain_hbm,
    one_ref, odd_near_ref, odd_far_ref, near_ref, far_ref, first_ref, last_ref, needs_ref, ids_ref, gain_ref, k_ref, v_ref, plan_ref,
    start_ref, sems,
):
    pairs = (start_hbm, start_ref), (ids_hbm, ids_ref), (k_hbm, k_ref), (v_hbm, v_ref), (gain_hbm, gain_ref)
    copies = [pltpu.make_async_copy(*pair, sems.at[i]) for i, pair in enumerate(pairs)]
    for copy in copies:
        copy.start()
    for copy in copies[:2]:
        copy.wait()
    me, top = lax.axis_index("seq"), start_ref.shape[0] - 1
    blocks, pairs = [jnp.int32(0), jnp.int32(0)], jnp.int32(0)
    for c in range(top + 1):
        begin = start_ref[c]
        plan_ref[1 + c] = begin
        blocks[c % 2] = jnp.maximum(blocks[c % 2], c - begin)
        pairs = jnp.maximum(pairs, c // 2 - (begin >> 1))
    even, odd = blocks
    by_pairs = jnp.where(pairs <= 2, PAIRS + (pairs - 1), ANY)
    by_shifts = jnp.where(even == 2, TWO, jnp.where(odd == 2, ODD, ONE))
    plan_ref[0] = jnp.where(jnp.maximum(even, odd) <= 2, by_shifts, by_pairs)
    for row, need in enumerate(backward_needs(start_ref, me) + pair_needs(start_ref, me, 1) + pair_needs(start_ref, me, -1)):
        needs_ref[row : row + 1, :] = jnp.full((1, HD), jnp.where(need, 1.0, 0.0), f32)
    need, need2 = [
        (me + step <= top) & (start_ref[jnp.minimum(me + step, top)] <= me) for step in (1, 2)
    ]
    row, col = ids_of(ids_ref)
    first_ref[...] = wide((col == row[:, :1]).astype(f32))
    last = (col == row[:, -1:]).astype(f32)
    last_ref[...] = wide(last)
    last = wide(last * jnp.where(need, 1.0, 0.0))
    for copy in copies[2:]:
        copy.wait()
    for h in range(one_ref.shape[0]):
        state = dot(k_ref[:, head_cols(h)] * last, v_ref[:, head_cols(h)], 0, 0)
        one_ref[h] = odd_near_ref[h] = near_ref[h] = state.astype(bf16)
        odd_far_ref[h] = far_ref[h] = jnp.where(need2, state, 0.0).astype(bf16)


def state_kernel(mask_ref, a_ref, b_ref, state_ref):
    mask = mask_ref[...]
    for h in range(state_ref.shape[0]):
        c = head_cols(h)
        state_ref[h] = dot(a_ref[:, c] * mask, b_ref[:, c], 0, 0).astype(bf16)


def local_kernel(plan, q_hbm, g_hbm, ids_ref, k_ref, v_ref, att_ref, q_ref, g_ref, sems):
    copies = [pltpu.make_async_copy(*pair, sems.at[i]) for i, pair in enumerate(((q_hbm, q_ref), (g_hbm, g_ref)))]
    for copy in copies:
        copy.start()
    row, col = ids_of(ids_ref)
    n = row.shape[1]
    t = lax.broadcasted_iota(jnp.int32, (n, n), 0)
    u = lax.broadcasted_iota(jnp.int32, (n, n), 1)
    same = (u <= t) & (col == row)
    for copy in copies:
        copy.wait()

    def head(h):
        c = head_cols(h)
        w = jnp.where(same, dot(q_ref[:, c], k_ref[:, c], 1, 1), 0.0).astype(bf16)
        att_ref[:, c] = dot(w, v_ref[:, c], 1, 0)

    each_head(plan, q_ref.shape[1] // HD, head)


def picked(needs_ref, row):
    return jnp.broadcast_to(needs_ref[row : row + 1, :], (HD, HD)) > 0.5


def chosen(picks, refs, h):
    return sum(jnp.where(pick, ref[h].astype(f32), 0.0) for pick, ref in zip(picks, refs)).astype(bf16)


def joined(plan, way, refs):
    if plan in (PAIRS, CHAIN):
        needs_ref, *refs = refs
        first = BACKWARD + (2 if way == 1 else 2 + PAIR)
        picks = [picked(needs_ref, first + i) for i in range(3)]
        return lambda h: chosen(picks, refs, h)
    return lambda h: refs[0][h] if len(refs) == 1 else refs[0][h] + refs[1][h]


def pair_kernel(way, needs_ref, own_ref, twin_ref, out_ref):
    first = BACKWARD + (0 if way == 1 else PAIR)
    picks = [picked(needs_ref, first + i) for i in range(2)]
    for h in range(out_ref.shape[0]):
        out_ref[h] = chosen(picks, (own_ref, twin_ref), h)


def chain_kernel(way, needs_ref, own_ref, inner_ref, outer_ref, out_ref):
    first = BACKWARD + (5 if way == 1 else 5 + PAIR)
    picks = [picked(needs_ref, first + i) for i in range(2)]
    for h in range(out_ref.shape[0]):
        out_ref[h] = own_ref[h] + chosen(picks, (inner_ref, outer_ref), h)


def attend_kernel(plan, first_ref, att_ref, q_ref, g_ref, gain_ref, *refs):
    state_refs, (out_ref, sums_ref) = refs[:-2], refs[-2:]
    first = first_ref[...]
    carry = joined(plan, 1, state_refs)
    square = jnp.zeros(first.shape, f32)
    cross = jnp.zeros(first.shape, f32)
    for h in range(q_ref.shape[1] // HD):
        c = head_cols(h)
        att = att_ref[:, c] + dot(q_ref[:, c] * first, carry(h), 1, 0)
        out_ref[:, c] = att
        square = square + att * att
        cross = cross + gain_ref[:, c] * g_ref[:, c].astype(f32) * att
    sums_ref[0:1, :] = as_row(jnp.sum(square, axis=1, keepdims=True))
    sums_ref[1:2, :] = as_row(jnp.sum(cross, axis=1, keepdims=True))


def scales(sum_refs):
    total = sum_refs[0][...]
    for ref in sum_refs[1:]:
        total = total + ref[...]
    inverse = lax.rsqrt(total[0:1] / WIDTH + epsilon)
    pull = inverse * inverse * inverse * total[1:2] / WIDTH
    return inverse, pull


def grad_kernel(n_heads, needs_ref, first_ref, att_ref, q_ref, g_ref, gain_ref, *refs):
    sum_refs, grad_ref, head_refs = refs[: -n_heads - 1], refs[-n_heads - 1], refs[-n_heads:]
    first = first_ref[...]
    needs = [picked(needs_ref, i) for i in range(n_heads)]
    inverse, pull = scales(sum_refs)
    inverse, pull = column(inverse), column(pull)
    for h in range(q_ref.shape[1] // HD):
        c = head_cols(h)
        grad = (inverse * gain_ref[:, c] * g_ref[:, c].astype(f32) - pull * att_ref[:, c]).astype(bf16)
        grad_ref[:, c] = grad
        state = dot(q_ref[:, c] * first, grad, 0, 0)
        for ref, need in zip(head_refs, needs):
            ref[h] = jnp.where(need, state, 0.0).astype(bf16)


def back_kernel(plan, n_sums, ids_ref, first_ref, att_ref, q_ref, k_ref, v_ref, grad_ref, gain_ref, *refs):
    sum_refs, state_refs, (normed_ref, gq_ref, gk_ref, gv_ref) = refs[:n_sums], refs[n_sums:-4], refs[-4:]
    inverse = column(scales(sum_refs)[0])
    carry = joined(plan, 1, state_refs)
    row, col = ids_of(ids_ref)
    first = first_ref[...]
    n = row.shape[1]
    t = lax.broadcasted_iota(jnp.int32, (n, n), 0)
    u = lax.broadcasted_iota(jnp.int32, (n, n), 1)
    same = (u <= t) & (col == row)
    same_t = (t <= u) & (col == row)

    def head(h):
        c = head_cols(h)
        q, k, v, grad = q_ref[:, c], k_ref[:, c], v_ref[:, c], grad_ref[:, c]
        normed_ref[:, c] = (att_ref[:, c] * inverse * gain_ref[:, c]).astype(bf16)
        gs = jnp.where(same, dot(grad, v, 1, 1), 0.0).astype(bf16)
        gq_ref[:, c] = (dot(gs, k, 1, 0) + dot(grad * first, carry(h), 1, 1)).astype(bf16)
        gs_t = jnp.where(same_t, dot(v, grad, 1, 1), 0.0).astype(bf16)
        gk_ref[:, c] = dot(gs_t, q, 1, 0)
        w_t = jnp.where(same_t, dot(k, q, 1, 1), 0.0).astype(bf16)
        gv_ref[:, c] = dot(w_t, grad, 1, 0)

    each_head(plan, q_ref.shape[1] // HD, head)


def add_kernel(last_ref, k_ref, v_ref, state_ref, gk_in, gv_in, gk_ref, gv_ref):
    last = last_ref[...]
    for h in range(k_ref.shape[1] // HD):
        c = head_cols(h)
        gk_ref[:, c] = gk_in[:, c] + dot(v_ref[:, c] * last, state_ref[h], 1, 1)
        gv_ref[:, c] = gv_in[:, c] + dot(k_ref[:, c] * last, state_ref[h], 1, 0)


def last_kernel(plan, last_ref, k_ref, v_ref, gk_in, gv_in, *refs):
    state_refs, (gk_hbm, gv_hbm, gk_ref, gv_ref, sems) = refs[:-5], refs[-5:]
    last = last_ref[...]
    back_of = joined(plan, -1, state_refs)
    chunks, _, cols = gk_ref.shape
    copies = []
    for i in range(chunks):
        for j in range(cols // HD):
            h = i * (cols // HD) + j
            c = head_cols(h)
            back = back_of(h)
            gk_ref[i, :, head_cols(j)] = (gk_in[:, c] + dot(v_ref[:, c] * last, back, 1, 1)).astype(bf16)
            gv_ref[i, :, head_cols(j)] = (gv_in[:, c] + dot(k_ref[:, c] * last, back, 1, 0)).astype(bf16)
        at = pl.ds(i * cols, cols)
        copies.append(pltpu.make_async_copy(gk_ref.at[i], gk_hbm.at[:, at], sems.at[2 * i]))
        copies.append(pltpu.make_async_copy(gv_ref.at[i], gv_hbm.at[:, at], sems.at[2 * i + 1]))
        copies[-2].start()
        copies[-1].start()
    for copy in copies:
        copy.wait()


def shape_of(a):
    return jax.ShapeDtypeStruct(a.shape, a.dtype)


def in_hbm(a):
    return pltpu.with_memory_space_constraint(a, pltpu.HBM)


def call(kernel, outs, flops, *args, in_space=None, out_space=None, scratch=()):
    moved = sum(a.size * a.dtype.itemsize for a in (*args, *outs))

    def spec(a, space):
        return pl.BlockSpec(memory_space=space or (pltpu.SMEM if len(a.shape) == 1 else pltpu.VMEM))

    return pl.pallas_call(
        kernel,
        out_shape=outs,
        in_specs=[spec(a, space) for a, space in zip(args, in_space or [None] * len(args))],
        out_specs=tuple(spec(a, out_space) for a in outs),
        scratch_shapes=scratch,
        cost_estimate=pl.CostEstimate(flops=flops, bytes_accessed=moved, transcendentals=0),
        compiler_params=pltpu.CompilerParams(vmem_limit_bytes=32 * 2**20),
    )(*args)


def spread(state, mask, groups):
    shape = state.shape
    pieces = state.reshape(groups, -1, shape[-1])
    here = lax.all_to_all(pieces, "seq", 0, 0)
    sums = jnp.einsum("cj,jmn->cmn", mask.astype(bf16), here, preferred_element_type=f32)
    return lax.all_to_all(sums.astype(bf16), "seq", 0, 0).reshape(shape)


def over_head(sums):
    size = lax.axis_size("head")
    power = size & (size - 1) == 0
    return [sums] + [
        lax.ppermute(sums, "head", [(i, i ^ k if power else (i + k) % size) for i in range(size)])
        for k in range(1, size)
    ]


def exchange(plan, way, states, needs, plan_and_start):
    groups = lax.axis_size("seq")
    if plan in (ONE, ODD, TWO):
        return [
            lax.ppermute(state, "seq", [
                (i, (i + way * k) % groups)
                for i in range(groups)
                if (0 <= i + way * k < groups and (k == 1 or plan == TWO or i % 2 == 1))
                or (plan != ONE and way == 1 and k == 1)
            ])
            for k, state in enumerate(states, 1)
        ]
    (state,) = states
    if plan in (PAIRS, CHAIN):
        ends = (0, 1, groups - 2, groups - 1)
        inner = [(i, i ^ 2) for i in range(groups)]
        outer = [(i, i ^ 1 if i in ends else ((i - 2) ^ 2) + 2) for i in range(groups)]

        def swapped(pairs):
            return lax.ppermute(given, "seq", pairs)

        twin = lax.ppermute(state, "seq", [(i, i ^ 1) for i in range(groups)])
        (given,) = call(functools.partial(pair_kernel, way), (shape_of(state),), 0, needs, state, twin)
        if plan == CHAIN:
            taken = swapped(inner), swapped(outer)
            (given,) = call(functools.partial(chain_kernel, way), (shape_of(state),), 0, needs, given, *taken)
        return [needs, twin, swapped(inner), swapped(outer)]
    start_group, ids = plan_and_start[1:], jnp.arange(groups, dtype=jnp.int32)
    reach = (start_group[:, None] <= ids[None, :]) & (ids[None, :] < ids[:, None])
    return [spread(state, reach if way == 1 else reach.T, groups)]


def layer(plan, one, odd_near, odd_far, near, far, first, last, needs, ids, gain, key_in, value_in, plan_and_start, query_in, out_grad):
    n, cols = query_in.shape
    heads = cols // HD
    tokens = shape_of(query_in)
    tokens32 = jax.ShapeDtypeStruct((n, cols), f32)
    square = 2 * heads * n * n * HD
    narrow = 2 * heads * n * HD * HD

    state = shape_of(one)
    tails = {ONE: [one], ODD: [odd_near, odd_far], TWO: [near, far]}.get(plan) or call(state_kernel, (state,), narrow, last, key_in, value_in)
    earlier = exchange(plan, 1, tails, needs, plan_and_start)
    att_local, query_in, out_grad = call(
        functools.partial(local_kernel, plan),
        (tokens32, tokens, tokens),
        2 * square,
        in_hbm(query_in), in_hbm(out_grad), ids, key_in, value_in,
        in_space=[pltpu.HBM] * 2 + [pltpu.VMEM] * 3,
        scratch=[pltpu.SemaphoreType.DMA((2,))],
    )
    att, sums = call(
        functools.partial(attend_kernel, plan),
        (tokens32, jax.ShapeDtypeStruct((2, n), f32)),
        narrow,
        first, att_local, query_in, out_grad, gain, *earlier,
    )
    sums = over_head(sums)
    n_heads = 2 if plan in (ODD, TWO) else 1
    grad, *head_states = call(
        functools.partial(grad_kernel, n_heads),
        (tokens, *[state] * n_heads),
        narrow,
        needs, first, att, query_in, out_grad, gain, *sums,
    )
    later = exchange(plan, -1, head_states, needs, plan_and_start)
    normed, grad_query, gk, gv = call(
        functools.partial(back_kernel, plan, len(sums)),
        (tokens, tokens, tokens32, tokens32),
        6 * square + narrow,
        ids, first, att, query_in, key_in, value_in, grad, gain, *sums, *earlier,
    )
    chunks = 4 if heads % 4 == 0 else 1
    part = pltpu.VMEM((chunks, n, cols // chunks), bf16)
    if plan == TWO:
        near, far = later
        gk, gv = call(add_kernel, (tokens32, tokens32), 2 * narrow, last, key_in, value_in, far, gk, gv)
        later = [near]
    grad_key, grad_value = call(
        functools.partial(last_kernel, plan),
        (tokens, tokens),
        2 * narrow,
        last, key_in, value_in, gk, gv, *later,
        out_space=pltpu.HBM,
        scratch=[part, part, pltpu.SemaphoreType.DMA((2 * chunks,))],
    )
    return normed, grad_query, grad_key, grad_value


def local(query_in, key_in, value_in, out_grad, norm_gain, doc_ids, start_group):
    n, cols = query_in.shape
    heads = cols // HD
    ids, gain = doc_ids.reshape(1, n), norm_gain.reshape(1, cols)
    state = jax.ShapeDtypeStruct((heads, HD, HD), bf16)
    mask = jax.ShapeDtypeStruct((n, HD), bf16)
    *held, plan = call(
        tail_kernel,
        (
            *[state] * 5, mask, mask,
            jax.ShapeDtypeStruct((BACKWARD + 2 * PAIR, HD), f32), shape_of(ids), shape_of(gain), shape_of(key_in), shape_of(value_in),
            jax.ShapeDtypeStruct((1 + start_group.shape[0],), jnp.int32),
        ),
        2 * heads * n * HD * HD,
        *map(in_hbm, (start_group, ids, key_in, value_in, gain)),
        in_space=[pltpu.HBM] * 5,
        scratch=[pltpu.SMEM(start_group.shape, jnp.int32), pltpu.SemaphoreType.DMA((5,))],
    )
    in_pairs = (PAIRS, CHAIN) if start_group.shape[0] % 4 == 0 else (ANY, ANY)
    plans = (ONE, ODD, TWO, *in_pairs, ANY)
    return lax.switch(
        plan[0],
        [functools.partial(layer, way) for way in plans],
        *held, plan, query_in, out_grad,
    )


def solution(mesh):
    block = P("seq", "head")
    return jax.shard_map(
        local,
        mesh=mesh,
        in_specs=(block, block, block, block, P("head"), P("seq"), P()),
        out_specs=(block, block, block, block),
        check_vma=False,
    )
```

```python
import functools

import jax
import jax.numpy as jnp
from jax import lax
from jax.experimental import pallas as pl
from jax.experimental.pallas import tpu as pltpu
from jax.sharding import PartitionSpec as P

H = 32
HD = 128
WIDTH = H * HD

epsilon = 1e-06

ONE, ODD, TWO, PAIRS, CHAIN, ANY = range(6)

f32 = jnp.float32
bf16 = jnp.bfloat16


def dot(a, b, da, db):
    return lax.dot_general(a, b, (((da,), (db,)), ((), ())), preferred_element_type=f32)


def head_cols(h):
    return slice(h * HD, (h + 1) * HD) if isinstance(h, int) else pl.ds(pl.multiple_of(h * HD, HD), HD)


def column(row):
    n = row.shape[1]
    at = lax.broadcasted_iota(jnp.int32, (n, n), 0) == lax.broadcasted_iota(jnp.int32, (n, n), 1)
    return jnp.sum(jnp.where(at, row, 0.0), axis=1, keepdims=True)


def as_row(col):
    n = col.shape[0]
    at = lax.broadcasted_iota(jnp.int32, (n, n), 0) == lax.broadcasted_iota(jnp.int32, (n, n), 1)
    return jnp.sum(jnp.where(at, col, 0.0), axis=0, keepdims=True)


def ids_of(ids_ref):
    row = ids_ref[...].astype(f32)
    return row, jnp.transpose(jnp.broadcast_to(row, (8, row.shape[1])))[:, :1]


def wide(col, dtype=bf16):
    return jnp.broadcast_to(col, (col.shape[0], HD)).astype(dtype)


BACKWARD, PAIR = 2, 7


def backward_needs(start_ref, me):
    return [start_ref[me] <= me - step for step in (1, 2)]


def pair_needs(start_ref, me, way):
    top = start_ref.shape[0] - 1
    pair, odd = me >> 1, me & 1
    if way == 1:
        both = start_ref[jnp.minimum(2 * pair + 2, top)] <= 2 * pair
        twin = (odd == 1) & (start_ref[me] < me)
        far = start_ref[me] < 2 * pair
        through = start_ref[jnp.minimum(2 * pair + 2, top)] < 2 * pair
    else:
        both = start_ref[jnp.minimum(2 * pair + 1, top)] < 2 * pair
        twin = (odd == 0) & (start_ref[jnp.minimum(me + 1, top)] <= me)
        beyond = jnp.minimum(2 * pair + 2, top)
        far = (2 * pair + 2 <= top) & (start_ref[beyond] <= me)
        through = (2 * pair + 2 <= top) & (start_ref[beyond] < 2 * pair)
    near = (odd == 1) == (way == 1)
    inner = (pair & 1 == 1) == (way == 1)
    outer = jnp.logical_not(inner)
    return [
        near | both, both | jnp.logical_not(near),
        twin, far & inner, far & outer,
        through & inner, through & outer,
    ]


def tail_kernel(
    start_hbm, ids_hbm, k_hbm, v_hbm, gain_hbm,
    one_ref, odd_near_ref, odd_far_ref, near_ref, far_ref, first_ref, last_ref, needs_ref, ids_ref, gain_ref, k_ref, v_ref, plan_ref,
    start_ref, sems,
):
    pairs = (start_hbm, start_ref), (ids_hbm, ids_ref), (k_hbm, k_ref), (v_hbm, v_ref), (gain_hbm, gain_ref)
    copies = [pltpu.make_async_copy(*pair, sems.at[i]) for i, pair in enumerate(pairs)]
    for copy in copies:
        copy.start()
    for copy in copies[:2]:
        copy.wait()
    me, top = lax.axis_index("seq"), start_ref.shape[0] - 1
    blocks, pairs = [jnp.int32(0), jnp.int32(0)], jnp.int32(0)
    for c in range(top + 1):
        begin = start_ref[c]
        plan_ref[1 + c] = begin
        blocks[c % 2] = jnp.maximum(blocks[c % 2], c - begin)
        pairs = jnp.maximum(pairs, c // 2 - (begin >> 1))
    even, odd = blocks
    by_pairs = jnp.where(pairs <= 2, PAIRS + (pairs - 1), ANY)
    by_shifts = jnp.where(even == 2, TWO, jnp.where(odd == 2, ODD, ONE))
    plan_ref[0] = jnp.where(jnp.maximum(even, odd) <= 2, by_shifts, by_pairs)
    for row, need in enumerate(backward_needs(start_ref, me) + pair_needs(start_ref, me, 1) + pair_needs(start_ref, me, -1)):
        needs_ref[row : row + 1, :] = jnp.full((1, HD), jnp.where(need, 1.0, 0.0), f32)
    need, need2 = [
        (me + step <= top) & (start_ref[jnp.minimum(me + step, top)] <= me) for step in (1, 2)
    ]
    row, col = ids_of(ids_ref)
    first_ref[...] = wide((col == row[:, :1]).astype(f32))
    last = (col == row[:, -1:]).astype(f32)
    last_ref[...] = wide(last)
    last = wide(last * jnp.where(need, 1.0, 0.0))
    for copy in copies[2:]:
        copy.wait()
    for h in range(one_ref.shape[0]):
        state = dot(k_ref[:, head_cols(h)] * last, v_ref[:, head_cols(h)], 0, 0)
        one_ref[h] = odd_near_ref[h] = near_ref[h] = state.astype(bf16)
        odd_far_ref[h] = far_ref[h] = jnp.where(need2, state, 0.0).astype(bf16)


def state_kernel(mask_ref, a_ref, b_ref, state_ref):
    mask = mask_ref[...]
    for h in range(state_ref.shape[0]):
        c = head_cols(h)
        state_ref[h] = dot(a_ref[:, c] * mask, b_ref[:, c], 0, 0).astype(bf16)


def local_kernel(q_hbm, g_hbm, ids_ref, k_ref, v_ref, att_ref, q_ref, g_ref, sems):
    copies = [pltpu.make_async_copy(*pair, sems.at[i]) for i, pair in enumerate(((q_hbm, q_ref), (g_hbm, g_ref)))]
    for copy in copies:
        copy.start()
    row, col = ids_of(ids_ref)
    n = row.shape[1]
    t = lax.broadcasted_iota(jnp.int32, (n, n), 0)
    u = lax.broadcasted_iota(jnp.int32, (n, n), 1)
    same = (u <= t) & (col == row)
    for copy in copies:
        copy.wait()

    def head(h):
        c = head_cols(h)
        w = jnp.where(same, dot(q_ref[:, c], k_ref[:, c], 1, 1), 0.0).astype(bf16)
        att_ref[:, c] = dot(w, v_ref[:, c], 1, 0)

    pl.loop(0, q_ref.shape[1] // HD)(head)


def picked(needs_ref, row):
    return jnp.broadcast_to(needs_ref[row : row + 1, :], (HD, HD)) > 0.5


def chosen(picks, refs, h):
    return sum(jnp.where(pick, ref[h].astype(f32), 0.0) for pick, ref in zip(picks, refs)).astype(bf16)


def joined(plan, way, refs):
    if plan in (PAIRS, CHAIN):
        needs_ref, *refs = refs
        first = BACKWARD + (2 if way == 1 else 2 + PAIR)
        picks = [picked(needs_ref, first + i) for i in range(3)]
        return lambda h: chosen(picks, refs, h)
    return lambda h: refs[0][h] if len(refs) == 1 else refs[0][h] + refs[1][h]


def pair_kernel(way, needs_ref, own_ref, twin_ref, out_ref):
    first = BACKWARD + (0 if way == 1 else PAIR)
    picks = [picked(needs_ref, first + i) for i in range(2)]
    for h in range(out_ref.shape[0]):
        out_ref[h] = chosen(picks, (own_ref, twin_ref), h)


def chain_kernel(way, needs_ref, own_ref, inner_ref, outer_ref, out_ref):
    first = BACKWARD + (5 if way == 1 else 5 + PAIR)
    picks = [picked(needs_ref, first + i) for i in range(2)]
    for h in range(out_ref.shape[0]):
        out_ref[h] = own_ref[h] + chosen(picks, (inner_ref, outer_ref), h)


def attend_kernel(plan, first_ref, att_ref, q_ref, g_ref, gain_ref, *refs):
    state_refs, (out_ref, sums_ref) = refs[:-2], refs[-2:]
    first = first_ref[...]
    carry = joined(plan, 1, state_refs)
    square = jnp.zeros(first.shape, f32)
    cross = jnp.zeros(first.shape, f32)
    for h in range(q_ref.shape[1] // HD):
        c = head_cols(h)
        att = att_ref[:, c] + dot(q_ref[:, c] * first, carry(h), 1, 0)
        out_ref[:, c] = att
        square = square + att * att
        cross = cross + gain_ref[:, c] * g_ref[:, c].astype(f32) * att
    sums_ref[0:1, :] = as_row(jnp.sum(square, axis=1, keepdims=True))
    sums_ref[1:2, :] = as_row(jnp.sum(cross, axis=1, keepdims=True))


def scales(sum_refs):
    total = sum_refs[0][...]
    for ref in sum_refs[1:]:
        total = total + ref[...]
    inverse = lax.rsqrt(total[0:1] / WIDTH + epsilon)
    pull = inverse * inverse * inverse * total[1:2] / WIDTH
    return inverse, pull


def grad_kernel(n_heads, needs_ref, first_ref, att_ref, q_ref, g_ref, gain_ref, *refs):
    sum_refs, grad_ref, head_refs = refs[: -n_heads - 1], refs[-n_heads - 1], refs[-n_heads:]
    first = first_ref[...]
    needs = [picked(needs_ref, i) for i in range(n_heads)]
    inverse, pull = scales(sum_refs)
    inverse, pull = column(inverse), column(pull)
    for h in range(q_ref.shape[1] // HD):
        c = head_cols(h)
        grad = (inverse * gain_ref[:, c] * g_ref[:, c].astype(f32) - pull * att_ref[:, c]).astype(bf16)
        grad_ref[:, c] = grad
        state = dot(q_ref[:, c] * first, grad, 0, 0)
        for ref, need in zip(head_refs, needs):
            ref[h] = jnp.where(need, state, 0.0).astype(bf16)


def back_kernel(plan, n_sums, ids_ref, first_ref, att_ref, q_ref, k_ref, v_ref, grad_ref, gain_ref, *refs):
    sum_refs, state_refs, (normed_ref, gq_ref, gk_ref, gv_ref) = refs[:n_sums], refs[n_sums:-4], refs[-4:]
    inverse = column(scales(sum_refs)[0])
    carry = joined(plan, 1, state_refs)
    row, col = ids_of(ids_ref)
    first = first_ref[...]
    n = row.shape[1]
    t = lax.broadcasted_iota(jnp.int32, (n, n), 0)
    u = lax.broadcasted_iota(jnp.int32, (n, n), 1)
    same = (u <= t) & (col == row)
    same_t = (t <= u) & (col == row)

    def head(h):
        c = head_cols(h)
        q, k, v, grad = q_ref[:, c], k_ref[:, c], v_ref[:, c], grad_ref[:, c]
        normed_ref[:, c] = (att_ref[:, c] * inverse * gain_ref[:, c]).astype(bf16)
        gs = jnp.where(same, dot(grad, v, 1, 1), 0.0).astype(bf16)
        gq_ref[:, c] = (dot(gs, k, 1, 0) + dot(grad * first, carry(h), 1, 1)).astype(bf16)
        gs_t = jnp.where(same_t, dot(v, grad, 1, 1), 0.0).astype(bf16)
        gk_ref[:, c] = dot(gs_t, q, 1, 0)
        w_t = jnp.where(same_t, dot(k, q, 1, 1), 0.0).astype(bf16)
        gv_ref[:, c] = dot(w_t, grad, 1, 0)

    pl.loop(0, q_ref.shape[1] // HD)(head)


def add_kernel(last_ref, k_ref, v_ref, state_ref, gk_in, gv_in, gk_ref, gv_ref):
    last = last_ref[...]
    for h in range(k_ref.shape[1] // HD):
        c = head_cols(h)
        gk_ref[:, c] = gk_in[:, c] + dot(v_ref[:, c] * last, state_ref[h], 1, 1)
        gv_ref[:, c] = gv_in[:, c] + dot(k_ref[:, c] * last, state_ref[h], 1, 0)


def last_kernel(plan, last_ref, k_ref, v_ref, gk_in, gv_in, *refs):
    state_refs, (gk_hbm, gv_hbm, gk_ref, gv_ref, sems) = refs[:-5], refs[-5:]
    last = last_ref[...]
    back_of = joined(plan, -1, state_refs)
    chunks, _, cols = gk_ref.shape
    copies = []
    for i in range(chunks):
        for j in range(cols // HD):
            h = i * (cols // HD) + j
            c = head_cols(h)
            back = back_of(h)
            gk_ref[i, :, head_cols(j)] = (gk_in[:, c] + dot(v_ref[:, c] * last, back, 1, 1)).astype(bf16)
            gv_ref[i, :, head_cols(j)] = (gv_in[:, c] + dot(k_ref[:, c] * last, back, 1, 0)).astype(bf16)
        at = pl.ds(i * cols, cols)
        copies.append(pltpu.make_async_copy(gk_ref.at[i], gk_hbm.at[:, at], sems.at[2 * i]))
        copies.append(pltpu.make_async_copy(gv_ref.at[i], gv_hbm.at[:, at], sems.at[2 * i + 1]))
        copies[-2].start()
        copies[-1].start()
    for copy in copies:
        copy.wait()


def shape_of(a):
    return jax.ShapeDtypeStruct(a.shape, a.dtype)


def in_hbm(a):
    return pltpu.with_memory_space_constraint(a, pltpu.HBM)


def call(kernel, outs, flops, *args, in_space=None, out_space=None, scratch=()):
    moved = sum(a.size * a.dtype.itemsize for a in (*args, *outs))

    def spec(a, space):
        return pl.BlockSpec(memory_space=space or (pltpu.SMEM if len(a.shape) == 1 else pltpu.VMEM))

    return pl.pallas_call(
        kernel,
        out_shape=outs,
        in_specs=[spec(a, space) for a, space in zip(args, in_space or [None] * len(args))],
        out_specs=tuple(spec(a, out_space) for a in outs),
        scratch_shapes=scratch,
        cost_estimate=pl.CostEstimate(flops=flops, bytes_accessed=moved, transcendentals=0),
        compiler_params=pltpu.CompilerParams(vmem_limit_bytes=32 * 2**20),
    )(*args)


def spread(state, mask, groups):
    shape = state.shape
    pieces = state.reshape(groups, -1, shape[-1])
    here = lax.all_to_all(pieces, "seq", 0, 0)
    sums = jnp.einsum("cj,jmn->cmn", mask.astype(bf16), here, preferred_element_type=f32)
    return lax.all_to_all(sums.astype(bf16), "seq", 0, 0).reshape(shape)


def over_head(sums):
    size = lax.axis_size("head")
    power = size & (size - 1) == 0
    return [sums] + [
        lax.ppermute(sums, "head", [(i, i ^ k if power else (i + k) % size) for i in range(size)])
        for k in range(1, size)
    ]


def exchange(plan, way, states, needs, plan_and_start):
    groups = lax.axis_size("seq")
    if plan in (ONE, ODD, TWO):
        return [
            lax.ppermute(state, "seq", [
                (i, (i + way * k) % groups)
                for i in range(groups)
                if (0 <= i + way * k < groups and (k == 1 or plan == TWO or i % 2 == 1))
                or (plan != ONE and way == 1 and k == 1)
            ])
            for k, state in enumerate(states, 1)
        ]
    (state,) = states
    if plan in (PAIRS, CHAIN):
        ends = (0, 1, groups - 2, groups - 1)
        inner = [(i, i ^ 2) for i in range(groups)]
        outer = [(i, i ^ 1 if i in ends else ((i - 2) ^ 2) + 2) for i in range(groups)]

        def swapped(pairs):
            return lax.ppermute(given, "seq", pairs)

        twin = lax.ppermute(state, "seq", [(i, i ^ 1) for i in range(groups)])
        (given,) = call(functools.partial(pair_kernel, way), (shape_of(state),), 0, needs, state, twin)
        if plan == CHAIN:
            taken = swapped(inner), swapped(outer)
            (given,) = call(functools.partial(chain_kernel, way), (shape_of(state),), 0, needs, given, *taken)
        return [needs, twin, swapped(inner), swapped(outer)]
    start_group, ids = plan_and_start[1:], jnp.arange(groups, dtype=jnp.int32)
    reach = (start_group[:, None] <= ids[None, :]) & (ids[None, :] < ids[:, None])
    return [spread(state, reach if way == 1 else reach.T, groups)]


def layer(plan, one, odd_near, odd_far, near, far, first, last, needs, ids, gain, key_in, value_in, plan_and_start, query_in, out_grad):
    n, cols = query_in.shape
    heads = cols // HD
    tokens = shape_of(query_in)
    tokens32 = jax.ShapeDtypeStruct((n, cols), f32)
    square = 2 * heads * n * n * HD
    narrow = 2 * heads * n * HD * HD

    state = shape_of(one)
    tails = {ONE: [one], ODD: [odd_near, odd_far], TWO: [near, far]}.get(plan) or call(state_kernel, (state,), narrow, last, key_in, value_in)
    earlier = exchange(plan, 1, tails, needs, plan_and_start)
    att_local, query_in, out_grad = call(
        local_kernel,
        (tokens32, tokens, tokens),
        2 * square,
        in_hbm(query_in), in_hbm(out_grad), ids, key_in, value_in,
        in_space=[pltpu.HBM] * 2 + [pltpu.VMEM] * 3,
        scratch=[pltpu.SemaphoreType.DMA((2,))],
    )
    att, sums = call(
        functools.partial(attend_kernel, plan),
        (tokens32, jax.ShapeDtypeStruct((2, n), f32)),
        narrow,
        first, att_local, query_in, out_grad, gain, *earlier,
    )
    sums = over_head(sums)
    n_heads = 2 if plan in (ODD, TWO) else 1
    grad, *head_states = call(
        functools.partial(grad_kernel, n_heads),
        (tokens, *[state] * n_heads),
        narrow,
        needs, first, att, query_in, out_grad, gain, *sums,
    )
    later = exchange(plan, -1, head_states, needs, plan_and_start)
    normed, grad_query, gk, gv = call(
        functools.partial(back_kernel, plan, len(sums)),
        (tokens, tokens, tokens32, tokens32),
        6 * square + narrow,
        ids, first, att, query_in, key_in, value_in, grad, gain, *sums, *earlier,
    )
    chunks = 4 if heads % 4 == 0 else 1
    part = pltpu.VMEM((chunks, n, cols // chunks), bf16)
    if plan == TWO:
        near, far = later
        gk, gv = call(add_kernel, (tokens32, tokens32), 2 * narrow, last, key_in, value_in, far, gk, gv)
        later = [near]
    grad_key, grad_value = call(
        functools.partial(last_kernel, plan),
        (tokens, tokens),
        2 * narrow,
        last, key_in, value_in, gk, gv, *later,
        out_space=pltpu.HBM,
        scratch=[part, part, pltpu.SemaphoreType.DMA((2 * chunks,))],
    )
    return normed, grad_query, grad_key, grad_value


def local(query_in, key_in, value_in, out_grad, norm_gain, doc_ids, start_group):
    n, cols = query_in.shape
    heads = cols // HD
    ids, gain = doc_ids.reshape(1, n), norm_gain.reshape(1, cols)
    state = jax.ShapeDtypeStruct((heads, HD, HD), bf16)
    mask = jax.ShapeDtypeStruct((n, HD), bf16)
    *held, plan = call(
        tail_kernel,
        (
            *[state] * 5, mask, mask,
            jax.ShapeDtypeStruct((BACKWARD + 2 * PAIR, HD), f32), shape_of(ids), shape_of(gain), shape_of(key_in), shape_of(value_in),
            jax.ShapeDtypeStruct((1 + start_group.shape[0],), jnp.int32),
        ),
        2 * heads * n * HD * HD,
        *map(in_hbm, (start_group, ids, key_in, value_in, gain)),
        in_space=[pltpu.HBM] * 5,
        scratch=[pltpu.SMEM(start_group.shape, jnp.int32), pltpu.SemaphoreType.DMA((5,))],
    )
    in_pairs = (PAIRS, CHAIN) if start_group.shape[0] % 4 == 0 else (ANY, ANY)
    plans = (ONE, ODD, TWO, *in_pairs, ANY)
    return lax.switch(
        plan[0],
        [functools.partial(layer, way) for way in plans],
        *held, plan, query_in, out_grad,
    )


def solution(mesh):
    block = P("seq", "head")
    return jax.shard_map(
        local,
        mesh=mesh,
        in_specs=(block, block, block, block, P("head"), P("seq"), P()),
        out_specs=(block, block, block, block),
        check_vma=False,
    )
```

```python
import functools

import jax
import jax.numpy as jnp
from jax import lax
from jax.experimental import pallas as pl
from jax.experimental.pallas import tpu as pltpu
from jax.sharding import PartitionSpec as P

H = 32
HD = 128
WIDTH = H * HD

epsilon = 1e-06

ONE, ODD, TWO, PAIRS, CHAIN, ANY = range(6)

f32 = jnp.float32
bf16 = jnp.bfloat16


def dot(a, b, da, db):
    return lax.dot_general(a, b, (((da,), (db,)), ((), ())), preferred_element_type=f32)


def head_cols(h):
    return slice(h * HD, (h + 1) * HD) if isinstance(h, int) else pl.ds(pl.multiple_of(h * HD, HD), HD)


def each_head(plan, heads, body):
    if plan in (PAIRS, CHAIN, ANY):
        pl.loop(0, heads)(body)
    else:
        for h in range(heads):
            body(h)


def column(row):
    n = row.shape[1]
    at = lax.broadcasted_iota(jnp.int32, (n, n), 0) == lax.broadcasted_iota(jnp.int32, (n, n), 1)
    return jnp.sum(jnp.where(at, row, 0.0), axis=1, keepdims=True)


def as_row(col):
    n = col.shape[0]
    at = lax.broadcasted_iota(jnp.int32, (n, n), 0) == lax.broadcasted_iota(jnp.int32, (n, n), 1)
    return jnp.sum(jnp.where(at, col, 0.0), axis=0, keepdims=True)


def ids_of(ids_ref):
    row = ids_ref[...].astype(f32)
    return row, column(row)


def wide(col, dtype=bf16):
    return jnp.broadcast_to(col, (col.shape[0], HD)).astype(dtype)


BACKWARD, PAIR = 2, 7


def backward_needs(start_ref, me):
    return [start_ref[me] <= me - step for step in (1, 2)]


def pair_needs(start_ref, me, way):
    top = start_ref.shape[0] - 1
    pair, odd = me >> 1, me & 1
    if way == 1:
        both = start_ref[jnp.minimum(2 * pair + 2, top)] <= 2 * pair
        twin = (odd == 1) & (start_ref[me] < me)
        far = start_ref[me] < 2 * pair
        through = start_ref[jnp.minimum(2 * pair + 2, top)] < 2 * pair
    else:
        both = start_ref[jnp.minimum(2 * pair + 1, top)] < 2 * pair
        twin = (odd == 0) & (start_ref[jnp.minimum(me + 1, top)] <= me)
        beyond = jnp.minimum(2 * pair + 2, top)
        far = (2 * pair + 2 <= top) & (start_ref[beyond] <= me)
        through = (2 * pair + 2 <= top) & (start_ref[beyond] < 2 * pair)
    near = (odd == 1) == (way == 1)
    inner = (pair & 1 == 1) == (way == 1)
    outer = jnp.logical_not(inner)
    return [
        near | both, both | jnp.logical_not(near),
        twin, far & inner, far & outer,
        through & inner, through & outer,
    ]


def tail_kernel(
    start_hbm, ids_hbm, k_hbm, v_hbm, gain_hbm,
    one_ref, odd_near_ref, odd_far_ref, near_ref, far_ref, first_ref, last_ref, needs_ref, ids_ref, gain_ref, k_ref, v_ref, plan_ref,
    start_ref, sems,
):
    pairs = (start_hbm, start_ref), (ids_hbm, ids_ref), (k_hbm, k_ref), (v_hbm, v_ref), (gain_hbm, gain_ref)
    copies = [pltpu.make_async_copy(*pair, sems.at[i]) for i, pair in enumerate(pairs)]
    for copy in copies:
        copy.start()
    for copy in copies[:2]:
        copy.wait()
    me, top = lax.axis_index("seq"), start_ref.shape[0] - 1
    blocks, pairs = [jnp.int32(0), jnp.int32(0)], jnp.int32(0)
    for c in range(top + 1):
        begin = start_ref[c]
        plan_ref[1 + c] = begin
        blocks[c % 2] = jnp.maximum(blocks[c % 2], c - begin)
        pairs = jnp.maximum(pairs, c // 2 - (begin >> 1))
    even, odd = blocks
    by_pairs = jnp.where(pairs <= 2, PAIRS + (pairs - 1), ANY)
    by_shifts = jnp.where(even == 2, TWO, jnp.where(odd == 2, ODD, ONE))
    plan_ref[0] = jnp.where(jnp.maximum(even, odd) <= 2, by_shifts, by_pairs)
    for row, need in enumerate(backward_needs(start_ref, me) + pair_needs(start_ref, me, 1) + pair_needs(start_ref, me, -1)):
        needs_ref[row : row + 1, :] = jnp.full((1, HD), jnp.where(need, 1.0, 0.0), f32)
    need, need2 = [
        (me + step <= top) & (start_ref[jnp.minimum(me + step, top)] <= me) for step in (1, 2)
    ]
    row = ids_ref[...].astype(f32)
    col = jnp.transpose(jnp.broadcast_to(row, (8, row.shape[1])))[:, :1]
    first_ref[...] = wide((col == row[:, :1]).astype(f32))
    last = (col == row[:, -1:]).astype(f32)
    last_ref[...] = wide(last)
    last = wide(last * jnp.where(need, 1.0, 0.0))
    for copy in copies[2:]:
        copy.wait()
    for h in range(one_ref.shape[0]):
        state = dot(k_ref[:, head_cols(h)] * last, v_ref[:, head_cols(h)], 0, 0)
        one_ref[h] = odd_near_ref[h] = near_ref[h] = state.astype(bf16)
        odd_far_ref[h] = far_ref[h] = jnp.where(need2, state, 0.0).astype(bf16)


def state_kernel(mask_ref, a_ref, b_ref, state_ref):
    mask = mask_ref[...]
    for h in range(state_ref.shape[0]):
        c = head_cols(h)
        state_ref[h] = dot(a_ref[:, c] * mask, b_ref[:, c], 0, 0).astype(bf16)


def local_kernel(plan, q_hbm, g_hbm, ids_ref, k_ref, v_ref, att_ref, q_ref, g_ref, sems):
    copies = [pltpu.make_async_copy(*pair, sems.at[i]) for i, pair in enumerate(((q_hbm, q_ref), (g_hbm, g_ref)))]
    for copy in copies:
        copy.start()
    row, col = ids_of(ids_ref)
    n = row.shape[1]
    t = lax.broadcasted_iota(jnp.int32, (n, n), 0)
    u = lax.broadcasted_iota(jnp.int32, (n, n), 1)
    same = (u <= t) & (col == row)
    for copy in copies:
        copy.wait()

    def head(h):
        c = head_cols(h)
        w = jnp.where(same, dot(q_ref[:, c], k_ref[:, c], 1, 1), 0.0).astype(bf16)
        att_ref[:, c] = dot(w, v_ref[:, c], 1, 0)

    each_head(plan, q_ref.shape[1] // HD, head)


def picked(needs_ref, row):
    return jnp.broadcast_to(needs_ref[row : row + 1, :], (HD, HD)) > 0.5


def chosen(picks, refs, h):
    return sum(jnp.where(pick, ref[h].astype(f32), 0.0) for pick, ref in zip(picks, refs)).astype(bf16)


def joined(plan, way, refs):
    if plan in (PAIRS, CHAIN):
        needs_ref, *refs = refs
        first = BACKWARD + (2 if way == 1 else 2 + PAIR)
        picks = [picked(needs_ref, first + i) for i in range(3)]
        return lambda h: chosen(picks, refs, h)
    return lambda h: refs[0][h] if len(refs) == 1 else refs[0][h] + refs[1][h]


def pair_kernel(way, needs_ref, own_ref, twin_ref, out_ref):
    first = BACKWARD + (0 if way == 1 else PAIR)
    picks = [picked(needs_ref, first + i) for i in range(2)]
    for h in range(out_ref.shape[0]):
        out_ref[h] = chosen(picks, (own_ref, twin_ref), h)


def chain_kernel(way, needs_ref, own_ref, inner_ref, outer_ref, out_ref):
    first = BACKWARD + (5 if way == 1 else 5 + PAIR)
    picks = [picked(needs_ref, first + i) for i in range(2)]
    for h in range(out_ref.shape[0]):
        out_ref[h] = own_ref[h] + chosen(picks, (inner_ref, outer_ref), h)


def attend_kernel(plan, first_ref, att_ref, q_ref, g_ref, gain_ref, *refs):
    state_refs, (out_ref, sums_ref) = refs[:-2], refs[-2:]
    first = first_ref[...]
    carry = joined(plan, 1, state_refs)
    square = jnp.zeros(first.shape, f32)
    cross = jnp.zeros(first.shape, f32)
    for h in range(q_ref.shape[1] // HD):
        c = head_cols(h)
        att = att_ref[:, c] + dot(q_ref[:, c] * first, carry(h), 1, 0)
        out_ref[:, c] = att
        square = square + att * att
        cross = cross + gain_ref[:, c] * g_ref[:, c].astype(f32) * att
    sums_ref[0:1, :] = as_row(jnp.sum(square, axis=1, keepdims=True))
    sums_ref[1:2, :] = as_row(jnp.sum(cross, axis=1, keepdims=True))


def scales(sum_refs):
    total = sum_refs[0][...]
    for ref in sum_refs[1:]:
        total = total + ref[...]
    inverse = lax.rsqrt(total[0:1] / WIDTH + epsilon)
    pull = inverse * inverse * inverse * total[1:2] / WIDTH
    return inverse, pull


def grad_kernel(n_heads, needs_ref, first_ref, att_ref, q_ref, g_ref, gain_ref, *refs):
    sum_refs, grad_ref, head_refs = refs[: -n_heads - 1], refs[-n_heads - 1], refs[-n_heads:]
    first = first_ref[...]
    needs = [picked(needs_ref, i) for i in range(n_heads)]
    inverse, pull = scales(sum_refs)
    inverse, pull = column(inverse), column(pull)
    for h in range(q_ref.shape[1] // HD):
        c = head_cols(h)
        grad = (inverse * gain_ref[:, c] * g_ref[:, c].astype(f32) - pull * att_ref[:, c]).astype(bf16)
        grad_ref[:, c] = grad
        state = dot(q_ref[:, c] * first, grad, 0, 0)
        for ref, need in zip(head_refs, needs):
            ref[h] = jnp.where(need, state, 0.0).astype(bf16)


def back_kernel(plan, n_sums, ids_ref, first_ref, att_ref, q_ref, k_ref, v_ref, grad_ref, gain_ref, *refs):
    sum_refs, state_refs, (normed_ref, gq_ref, gk_ref, gv_ref) = refs[:n_sums], refs[n_sums:-4], refs[-4:]
    inverse = column(scales(sum_refs)[0])
    carry = joined(plan, 1, state_refs)
    row, col = ids_of(ids_ref)
    first = first_ref[...]
    n = row.shape[1]
    t = lax.broadcasted_iota(jnp.int32, (n, n), 0)
    u = lax.broadcasted_iota(jnp.int32, (n, n), 1)
    same = (u <= t) & (col == row)
    same_t = (t <= u) & (col == row)

    def head(h):
        c = head_cols(h)
        q, k, v, grad = q_ref[:, c], k_ref[:, c], v_ref[:, c], grad_ref[:, c]
        normed_ref[:, c] = (att_ref[:, c] * inverse * gain_ref[:, c]).astype(bf16)
        gs = jnp.where(same, dot(grad, v, 1, 1), 0.0).astype(bf16)
        gq_ref[:, c] = (dot(gs, k, 1, 0) + dot(grad * first, carry(h), 1, 1)).astype(bf16)
        gs_t = jnp.where(same_t, dot(v, grad, 1, 1), 0.0).astype(bf16)
        gk_ref[:, c] = dot(gs_t, q, 1, 0)
        w_t = jnp.where(same_t, dot(k, q, 1, 1), 0.0).astype(bf16)
        gv_ref[:, c] = dot(w_t, grad, 1, 0)

    each_head(plan, q_ref.shape[1] // HD, head)


def add_kernel(last_ref, k_ref, v_ref, state_ref, gk_in, gv_in, gk_ref, gv_ref):
    last = last_ref[...]
    for h in range(k_ref.shape[1] // HD):
        c = head_cols(h)
        gk_ref[:, c] = gk_in[:, c] + dot(v_ref[:, c] * last, state_ref[h], 1, 1)
        gv_ref[:, c] = gv_in[:, c] + dot(k_ref[:, c] * last, state_ref[h], 1, 0)


def last_kernel(plan, last_ref, k_ref, v_ref, gk_in, gv_in, *refs):
    state_refs, (gk_hbm, gv_hbm, gk_ref, gv_ref, sems) = refs[:-5], refs[-5:]
    last = last_ref[...]
    back_of = joined(plan, -1, state_refs)
    chunks, _, cols = gk_ref.shape
    copies = []
    for i in range(chunks):
        for j in range(cols // HD):
            h = i * (cols // HD) + j
            c = head_cols(h)
            back = back_of(h)
            gk_ref[i, :, head_cols(j)] = (gk_in[:, c] + dot(v_ref[:, c] * last, back, 1, 1)).astype(bf16)
            gv_ref[i, :, head_cols(j)] = (gv_in[:, c] + dot(k_ref[:, c] * last, back, 1, 0)).astype(bf16)
        at = pl.ds(i * cols, cols)
        copies.append(pltpu.make_async_copy(gk_ref.at[i], gk_hbm.at[:, at], sems.at[2 * i]))
        copies.append(pltpu.make_async_copy(gv_ref.at[i], gv_hbm.at[:, at], sems.at[2 * i + 1]))
        copies[-2].start()
        copies[-1].start()
    for copy in copies:
        copy.wait()


def shape_of(a):
    return jax.ShapeDtypeStruct(a.shape, a.dtype)


def in_hbm(a):
    return pltpu.with_memory_space_constraint(a, pltpu.HBM)


def call(kernel, outs, flops, *args, in_space=None, out_space=None, scratch=()):
    moved = sum(a.size * a.dtype.itemsize for a in (*args, *outs))

    def spec(a, space):
        return pl.BlockSpec(memory_space=space or (pltpu.SMEM if len(a.shape) == 1 else pltpu.VMEM))

    return pl.pallas_call(
        kernel,
        out_shape=outs,
        in_specs=[spec(a, space) for a, space in zip(args, in_space or [None] * len(args))],
        out_specs=tuple(spec(a, out_space) for a in outs),
        scratch_shapes=scratch,
        cost_estimate=pl.CostEstimate(flops=flops, bytes_accessed=moved, transcendentals=0),
        compiler_params=pltpu.CompilerParams(vmem_limit_bytes=32 * 2**20),
    )(*args)


def spread(state, mask, groups):
    shape = state.shape
    pieces = state.reshape(groups, -1, shape[-1])
    here = lax.all_to_all(pieces, "seq", 0, 0)
    sums = jnp.einsum("cj,jmn->cmn", mask.astype(bf16), here, preferred_element_type=f32)
    return lax.all_to_all(sums.astype(bf16), "seq", 0, 0).reshape(shape)


def over_head(sums):
    size = lax.axis_size("head")
    power = size & (size - 1) == 0
    return [sums] + [
        lax.ppermute(sums, "head", [(i, i ^ k if power else (i + k) % size) for i in range(size)])
        for k in range(1, size)
    ]


def exchange(plan, way, states, needs, plan_and_start):
    groups = lax.axis_size("seq")
    if plan in (ONE, ODD, TWO):
        return [
            lax.ppermute(state, "seq", [
                (i, (i + way * k) % groups)
                for i in range(groups)
                if (0 <= i + way * k < groups and (k == 1 or plan == TWO or i % 2 == 1))
                or (plan != ONE and way == 1 and k == 1)
            ])
            for k, state in enumerate(states, 1)
        ]
    (state,) = states
    if plan in (PAIRS, CHAIN):
        ends = (0, 1, groups - 2, groups - 1)
        inner = [(i, i ^ 2) for i in range(groups)]
        outer = [(i, i ^ 1 if i in ends else ((i - 2) ^ 2) + 2) for i in range(groups)]

        def swapped(pairs):
            return lax.ppermute(given, "seq", pairs)

        twin = lax.ppermute(state, "seq", [(i, i ^ 1) for i in range(groups)])
        (given,) = call(functools.partial(pair_kernel, way), (shape_of(state),), 0, needs, state, twin)
        if plan == CHAIN:
            taken = swapped(inner), swapped(outer)
            (given,) = call(functools.partial(chain_kernel, way), (shape_of(state),), 0, needs, given, *taken)
        return [needs, twin, swapped(inner), swapped(outer)]
    start_group, ids = plan_and_start[1:], jnp.arange(groups, dtype=jnp.int32)
    reach = (start_group[:, None] <= ids[None, :]) & (ids[None, :] < ids[:, None])
    return [spread(state, reach if way == 1 else reach.T, groups)]


def layer(plan, one, odd_near, odd_far, near, far, first, last, needs, ids, gain, key_in, value_in, plan_and_start, query_in, out_grad):
    n, cols = query_in.shape
    heads = cols // HD
    tokens = shape_of(query_in)
    tokens32 = jax.ShapeDtypeStruct((n, cols), f32)
    square = 2 * heads * n * n * HD
    narrow = 2 * heads * n * HD * HD

    state = shape_of(one)
    tails = {ONE: [one], ODD: [odd_near, odd_far], TWO: [near, far]}.get(plan) or call(state_kernel, (state,), narrow, last, key_in, value_in)
    earlier = exchange(plan, 1, tails, needs, plan_and_start)
    att_local, query_in, out_grad = call(
        functools.partial(local_kernel, plan),
        (tokens32, tokens, tokens),
        2 * square,
        in_hbm(query_in), in_hbm(out_grad), ids, key_in, value_in,
        in_space=[pltpu.HBM] * 2 + [pltpu.VMEM] * 3,
        scratch=[pltpu.SemaphoreType.DMA((2,))],
    )
    att, sums = call(
        functools.partial(attend_kernel, plan),
        (tokens32, jax.ShapeDtypeStruct((2, n), f32)),
        narrow,
        first, att_local, query_in, out_grad, gain, *earlier,
    )
    sums = over_head(sums)
    n_heads = 2 if plan in (ODD, TWO) else 1
    grad, *head_states = call(
        functools.partial(grad_kernel, n_heads),
        (tokens, *[state] * n_heads),
        narrow,
        needs, first, att, query_in, out_grad, gain, *sums,
    )
    later = exchange(plan, -1, head_states, needs, plan_and_start)
    normed, grad_query, gk, gv = call(
        functools.partial(back_kernel, plan, len(sums)),
        (tokens, tokens, tokens32, tokens32),
        6 * square + narrow,
        ids, first, att, query_in, key_in, value_in, grad, gain, *sums, *earlier,
    )
    chunks = 4 if heads % 4 == 0 else 1
    part = pltpu.VMEM((chunks, n, cols // chunks), bf16)
    if plan == TWO:
        near, far = later
        gk, gv = call(add_kernel, (tokens32, tokens32), 2 * narrow, last, key_in, value_in, far, gk, gv)
        later = [near]
    grad_key, grad_value = call(
        functools.partial(last_kernel, plan),
        (tokens, tokens),
        2 * narrow,
        last, key_in, value_in, gk, gv, *later,
        out_space=pltpu.HBM,
        scratch=[part, part, pltpu.SemaphoreType.DMA((2 * chunks,))],
    )
    return normed, grad_query, grad_key, grad_value


def local(query_in, key_in, value_in, out_grad, norm_gain, doc_ids, start_group):
    n, cols = query_in.shape
    heads = cols // HD
    ids, gain = doc_ids.reshape(1, n), norm_gain.reshape(1, cols)
    state = jax.ShapeDtypeStruct((heads, HD, HD), bf16)
    mask = jax.ShapeDtypeStruct((n, HD), bf16)
    *held, plan = call(
        tail_kernel,
        (
            *[state] * 5, mask, mask,
            jax.ShapeDtypeStruct((BACKWARD + 2 * PAIR, HD), f32), shape_of(ids), shape_of(gain), shape_of(key_in), shape_of(value_in),
            jax.ShapeDtypeStruct((1 + start_group.shape[0],), jnp.int32),
        ),
        2 * heads * n * HD * HD,
        *map(in_hbm, (start_group, ids, key_in, value_in, gain)),
        in_space=[pltpu.HBM] * 5,
        scratch=[pltpu.SMEM(start_group.shape, jnp.int32), pltpu.SemaphoreType.DMA((5,))],
    )
    in_pairs = (PAIRS, CHAIN) if start_group.shape[0] % 4 == 0 else (ANY, ANY)
    plans = (ONE, ODD, TWO, *in_pairs, ANY)
    return lax.switch(
        plan[0],
        [functools.partial(layer, way) for way in plans],
        *held, plan, query_in, out_grad,
    )


def solution(mesh):
    block = P("seq", "head")
    return jax.shard_map(
        local,
        mesh=mesh,
        in_specs=(block, block, block, block, P("head"), P("seq"), P()),
        out_specs=(block, block, block, block),
        check_vma=False,
    )
```
